256 devices in a mesh: hid: 4 (over y), blk: 64 (over x, z, core).
Axes of the slice: x: 4, y: 4, z: 8, core: 2. Of those that a mesh axis runs over, the one named last changes fastest.
Arguments:
- features: bfloat16 [16384, 4096], P('blk', 'hid'), may hold values from -6 to 6
- coarse_weight: bfloat16 [4096, 4096], P('hid', 'blk'), may hold values from -0.25 to 0.25
- fine_weight: bfloat16 [512, 4096, 256], P('blk', 'hid'), may hold values from -0.25 to 0.25
- block_cluster: int32 [512], replicated, may hold values from 0 to 4095
- routes: int32 [16384, 8], P('blk'), may hold values from 0 to 511, as said below
- target_route: int32 [16384], P('blk'), may hold values from 0 to 7
- target_offset: int32 [16384], P('blk'), may hold values from 0 to 255
Outputs:
- row_loss: float32 [16384], P('blk')
- block_prob: float32 [16384, 8], P('blk')
The draws below stay inside these ranges and needn't reach their ends.
Inputs may be any that keep to these rules, and one draw needn't show every extreme that they name: `routes`: each row lists 8 different blocks; among the 256 rows of one index of blk (aligned blocks of rows) no block is listed by more than 8 rows and some block is listed by exactly 8 of them; among those rows the 8 blocks of one index of blk are listed 48 times in all at the most, and exactly 48 times for some index.
All inputs are finite; a program needn't handle non-finite values.
Results may differ from the reference program's by a relative error of at most 0.0003.
Values may be sent and summed in bfloat16 or wider, within the bound.
No kernel may reach another device: no remote copies, remote signals or barrier semaphores. Data moves between devices by JAX's collectives and lax.ppermute only.
A program may use at most 128 MiB of HBM per device.

```python
import jax
import jax.numpy as jnp
from jax import lax

D = 4096
C = 4096
LBL = 256
BLK_DEV = 8
TOP = 8
R_DEV = 256
NBLK = 512
CAP = 8
ROWS = 16384
N_BLK = 64


def group_routes(group_key):
    mean_load = R_DEV * TOP // N_BLK
    keys = jax.random.split(group_key, 5)
    device_rank = jax.random.permutation(keys[0], N_BLK)
    device_load = jnp.where(device_rank < N_BLK // 2, 3 * mean_load // 2, mean_load // 2).astype(jnp.int32)
    limits = jax.random.randint(keys[1], (N_BLK, BLK_DEV), (3 * CAP + 3) // 4, CAP + 1).astype(jnp.int32)
    limits = limits.at[:, 0].set(CAP)
    before = jnp.cumsum(limits, axis=1) - limits
    loads = jnp.clip(device_load[:, None] - before, 0, limits).astype(jnp.int32)
    local_order = jax.vmap(lambda k: jax.random.permutation(k, BLK_DEV))(jax.random.split(keys[2], N_BLK))
    device_ids = jnp.arange(N_BLK, dtype=jnp.int32)[:, None]
    block_loads = jnp.zeros((N_BLK, BLK_DEV), jnp.int32).at[device_ids, local_order].set(loads).reshape(-1)
    ends = jnp.cumsum(block_loads)
    pair_block = jnp.searchsorted(ends, jnp.arange(R_DEV * TOP, dtype=jnp.int32), side='right').astype(jnp.int32)
    table = pair_block.reshape(TOP, R_DEV).T
    table = table[jax.random.permutation(keys[3], R_DEV)]
    table = jax.vmap(lambda k, line: jax.random.permutation(k, line))(jax.random.split(keys[4], R_DEV), table)
    return table


def draw_routes(key, part):
    key = jax.random.fold_in(key, 11)
    group_keys = jax.random.split(key, N_BLK)
    return jax.vmap(group_routes)(group_keys).reshape(ROWS, TOP).astype(jnp.int32)


def plant(result, own_key, smallest, top_value):
    extent = result.shape
    spot = [jax.random.randint(jax.random.fold_in(own_key, axis), (), 0, extent[axis]) for axis in range(len(extent))]
    result = result.at[tuple(spot)].set(smallest)
    longest = extent.index(max(extent))
    spot[longest] = (spot[longest] + 1) % extent[longest]
    return result.at[tuple(spot)].set(top_value)


def shard_levels(key, dims, pieces, smallest, high):
    level = 1.0
    for position, blocks in pieces:
        steps = jax.random.uniform(jax.random.fold_in(jax.random.fold_in(key, 6), position), (blocks,), jnp.float32, smallest / len(pieces), high / len(pieces))
        level = level * jnp.repeat(jnp.exp(steps), dims[position] // blocks).reshape((-1,) + (1,) * (len(dims) - 1 - position))
    return level


def noise(own_key, extent, deviation, most, shards=(), kind=jnp.bfloat16):
    array = deviation * jax.random.normal(own_key, extent, jnp.float32)
    if shards:
        array = array * shard_levels(own_key, extent, shards, -0.22, 0.18)
    return jnp.clip(array, -most, most).astype(kind)


def setup_inputs(seed: int = 0) -> dict:
    splits = jax.random.split(jax.random.key(seed), 8)
    return {
        "features": noise(splits[0], (ROWS, D), 1.0, 6.0, ((0, 64), (1, 4))),
        "coarse_weight": noise(splits[1], (D, C), (D // 9) ** -0.5, 0.25, ((0, 4), (1, 64))),
        "fine_weight": noise(splits[2], (NBLK, D, LBL), (D // 9) ** -0.5, 0.25, ((0, 64), (1, 4))),
        "block_cluster": plant(jax.random.randint(splits[3], (NBLK,), 0, C), jax.random.fold_in(splits[3], 1), 0, C - 1).astype(jnp.int32),
        "routes": draw_routes(jax.random.fold_in(splits[7], 71), 0),
        "target_route": plant(jax.random.randint(splits[5], (ROWS,), 0, TOP), jax.random.fold_in(splits[5], 1), 0, TOP - 1).astype(jnp.int32),
        "target_offset": plant(jax.random.randint(splits[6], (ROWS,), 0, LBL), jax.random.fold_in(splits[6], 1), 0, LBL - 1).astype(jnp.int32),
    }


def pair_slots(route_rows, capacity):
    blocks_flat = route_rows.reshape(-1).astype(jnp.int32)
    count = blocks_flat.shape[0]
    sort_order = jnp.argsort(blocks_flat, stable=True).astype(jnp.int32)
    sorted_blocks = blocks_flat[sort_order]
    starts = jnp.searchsorted(sorted_blocks, sorted_blocks, side="left").astype(jnp.int32)
    rank_sorted = jnp.arange(count, dtype=jnp.int32) - starts
    rank_pairs = jnp.zeros((count,), jnp.int32).at[sort_order].set(rank_sorted)
    return blocks_flat * capacity + rank_pairs


def pair_offsets(target_route, target_offset, width):
    is_target = jnp.arange(width, dtype=jnp.int32)[None, :] == target_route[:, None]
    return jnp.where(is_target, target_offset[:, None], -1).reshape(-1).astype(jnp.int32)


def block_scores(logits, offsets):
    block_mass = jax.nn.logsumexp(logits, axis=-1)
    label_index = jnp.arange(logits.shape[-1], dtype=jnp.int32)
    target_value = jnp.sum(jnp.where(label_index == offsets[..., None], logits, 0.0), axis=-1)
    return block_mass, target_value


def finish(pair_mass, target_logit, coarse_pick):
    fine_lse = jax.nn.logsumexp(pair_mass, axis=1)
    log_prob = pair_mass - fine_lse[:, None]
    block_prob = jnp.exp(log_prob)
    row_loss = fine_lse - target_logit + jnp.sum(block_prob * (log_prob - coarse_pick), axis=1)
    return row_loss, block_prob


def reference(features, coarse_weight, fine_weight, block_cluster, routes, target_route, target_offset):
    coarse = jnp.dot(features, coarse_weight, preferred_element_type=jnp.float32)
    coarse_lse = jax.nn.logsumexp(coarse, axis=1)
    route_cluster = block_cluster[routes].astype(jnp.int32)
    coarse_pick = jnp.take_along_axis(coarse, route_cluster, axis=1) - coarse_lse[:, None]
    route_groups = routes.reshape(N_BLK, R_DEV, TOP)
    slot_index = jax.vmap(lambda group: pair_slots(group, CAP))(route_groups)
    offset_pairs = jax.vmap(lambda picks, places: pair_offsets(picks, places, TOP))(
        target_route.reshape(N_BLK, R_DEV), target_offset.reshape(N_BLK, R_DEV))
    source = jnp.arange(N_BLK, dtype=jnp.int32)[:, None]
    pair_number = jnp.broadcast_to(jnp.arange(R_DEV * TOP, dtype=jnp.int32)[None, :], (N_BLK, R_DEV * TOP))
    global_row = source * R_DEV + pair_number // TOP
    row_table = jnp.zeros((N_BLK, NBLK * CAP), jnp.int32).at[source, slot_index].set(global_row)
    offset_table = jnp.full((N_BLK, NBLK * CAP), -1, jnp.int32).at[source, slot_index].set(offset_pairs)

    def one_block(block_id):
        row_ids = lax.dynamic_slice_in_dim(row_table, block_id * CAP, CAP, 1).reshape(-1)
        offsets = lax.dynamic_slice_in_dim(offset_table, block_id * CAP, CAP, 1).reshape(-1)
        picked_rows = features[row_ids]
        weight_block = lax.dynamic_index_in_dim(fine_weight, block_id, 0, keepdims=False)
        logits = jnp.dot(picked_rows, weight_block, preferred_element_type=jnp.float32)
        return block_scores(logits, offsets)

    masses, targets = lax.map(one_block, jnp.arange(NBLK, dtype=jnp.int32))
    masses = masses.reshape(NBLK, N_BLK, CAP).transpose(1, 0, 2).reshape(N_BLK, NBLK * CAP)
    targets = targets.reshape(NBLK, N_BLK, CAP).transpose(1, 0, 2).reshape(N_BLK, NBLK * CAP)
    pair_mass = jnp.take_along_axis(masses, slot_index, axis=1).reshape(N_BLK * R_DEV, TOP)
    target_logit = jnp.sum(jnp.take_along_axis(targets, slot_index, axis=1).reshape(N_BLK * R_DEV, TOP), axis=1)
    row_loss, block_prob = finish(pair_mass, target_logit, coarse_pick)
    return row_loss, block_prob
```

```python
import jax
import jax.numpy as jnp
from jax import lax
from jax.experimental import pallas as pl
from jax.experimental.pallas import tpu as pltpu
from jax.sharding import Mesh, PartitionSpec as P

F32 = jnp.float32
BF16 = jnp.bfloat16
I32 = jnp.int32

HID, NX, NZ, NC = 4, 4, 8, 2
ROWS = 256
PART = 1024
TOP = 8
BLK = 8
QB = NC * BLK
CAP = 8
LBL = 256
INFO = 16
EXT = ROWS + INFO
VMEM = 56 * 1024 * 1024


def iota(shape, dim):
    return lax.broadcasted_iota(I32, shape, dim)


def dot(a, b):
    return jnp.dot(a, b, preferred_element_type=F32)


def strict_upper():
    return jnp.where(iota((ROWS, ROWS), 0) < iota((ROWS, ROWS), 1), 1.0, 0.0).astype(BF16)


def other(core, half):
    return core + half - 2 * core * half


def pack_kernel(f_ref, routes_ref, place_ref, table_ref, out_ref):
    out_ref[0:ROWS, :] = f_ref[...]
    routes = routes_ref[...]
    groups, columns = [], []
    blocks = iota((table_ref.shape[1], ROWS), 0)
    for k in range(TOP):
        hot = jnp.where(blocks == routes[k : k + 1, :], 1.0, 0.0).astype(BF16)
        found = dot(table_ref[...], hot)
        groups.append(found[0:1, :])
        columns.append(found[1:2, :])
    info = jnp.concatenate(
        [
            (routes - 256).astype(F32),
            jnp.concatenate(groups, axis=0),
            jnp.concatenate(columns, axis=0),
            place_ref[...].astype(F32),
        ],
        axis=1,
    )
    info = jnp.concatenate([info, jnp.zeros((INFO - TOP, PART), F32)], axis=0)
    out_ref[ROWS:EXT, :] = info.astype(BF16)


def select_kernel(at_ref, g_ref, w_ref, rows_ref, coarse_ref, offset_ref):
    step = pl.program_id(0)
    x, z, core = at_ref[0], at_ref[1], at_ref[2]
    count = NX * QB
    index = iota((count, ROWS), 0)
    device = (index >> 4) * (NZ * NC) + z * NC + other(core, (index >> 3) & 1)
    blocks = device * BLK + (index & 7)
    upper = strict_upper()
    spread = jnp.where(
        (iota((count * CAP, count), 0) >> 3) == iota((count * CAP, count), 1), 1.0, 0.0
    ).astype(BF16)
    rank_of = iota((count * CAP, ROWS), 0) & 7
    lane = iota((count, ROWS), 1)

    @pl.when(step == 0)
    def _():
        offset_ref[...] = jnp.zeros_like(offset_ref)

    offsets = offset_ref[...]
    hots = []
    for s in range(2):
        info = g_ref[s, ROWS:EXT, :].astype(F32)
        routes = info[0:TOP, 0:ROWS].astype(I32) + 256
        place = info[0:1, 3 * ROWS : 4 * ROWS].astype(I32)
        offset = info[1:2, 3 * ROWS : 4 * ROWS]
        hit = jnp.zeros((count, ROWS), F32)
        target = jnp.zeros((1, ROWS), I32)
        for k in range(TOP):
            hit = jnp.where(routes[k : k + 1, :] == blocks, 1.0, hit)
            target = jnp.where(place == k, routes[k : k + 1, :], target)
        rank = dot(hit.astype(BF16), upper)
        slot = jnp.where(hit > 0.5, rank, -1.0)
        value = jnp.where(blocks == target, offset + 1.0, 0.0)
        base = x * (NZ * CAP) + (2 * step + s) * CAP
        for r in range(CAP):
            column = jnp.sum(jnp.where(slot == float(r), value, 0.0), axis=1, keepdims=True)
            offsets = jnp.where(lane == base + r, column, offsets)
        wide = dot(spread, slot.astype(BF16)).astype(I32)
        hots.append(jnp.where(wide == rank_of, 1.0, 0.0).astype(BF16))
    offset_ref[...] = offsets
    part = QB * CAP
    for d in range(NX):
        picked = [
            dot(hots[s][d * part : (d + 1) * part, :], g_ref[s, 0:ROWS, :]).reshape(QB, CAP, PART)
            for s in range(2)
        ]
        rows_ref[d] = jnp.concatenate(picked, axis=1).astype(BF16)
    for s in range(2):
        coarse_ref[:, s * ROWS : (s + 1) * ROWS] = lax.dot_general(
            w_ref[...], g_ref[s, 0:ROWS, :], (((1,), (1,)), ((), ())), preferred_element_type=F32
        )


def fine_kernel(r_ref, own_ref, peer_ref, out_ref):
    block = pl.program_id(0)
    rows = r_ref[:, 0].reshape(NX * NZ * CAP, PART)

    @pl.when(block < BLK)
    def _():
        out_ref[0] = dot(rows, own_ref[0])

    @pl.when(block >= BLK)
    def _():
        out_ref[0] = dot(rows, peer_ref[0])


def score_kernel(at_ref, y_ref, offset_ref, out_ref):
    h = at_ref[3]
    slots = NX * NZ * CAP
    eye = iota((slots, slots), 0) == iota((slots, slots), 1)
    label = iota((slots, LBL), 1).astype(F32) + 1.0
    lane = iota((slots, 128), 1)
    first = (iota((slots, 128), 0) & 7) * 8
    packed = jnp.zeros((slots, 128), F32)
    for b in range(QB // HID):
        y = y_ref[b]
        row = jnp.zeros((1, slots), F32)
        for d in range(NX):
            row = row + offset_ref[d, pl.ds(h * (QB // HID) + b, 1), :]
        column = jnp.sum(jnp.where(eye, row, 0.0), axis=1, keepdims=True)
        top = jnp.max(y, axis=1, keepdims=True)
        mass = top + jnp.log(jnp.sum(jnp.exp(y - top), axis=1, keepdims=True))
        target = jnp.sum(jnp.where(label == column, y, 0.0), axis=1, keepdims=True)
        packed = jnp.where(lane == first + b, mass, packed)
        packed = jnp.where(lane == first + (4 + b), target, packed)
    packed = jnp.sum(packed.reshape(NX * NZ, CAP, 128), axis=1)
    for d in range(HID):
        out_ref[d] = packed


def coarse_kernel(at_ref, c_ref, info_ref, out_ref):
    z, h = at_ref[1], at_ref[3]
    logits = c_ref[...]
    width = logits.shape[0]
    info = info_ref[0].astype(F32).astype(I32)
    group = info[0:TOP, ROWS : 2 * ROWS]
    inside = info[0:TOP, 2 * ROWS : 3 * ROWS]
    place = ((group >> 4) * NC + (group & 1)) * 64 + inside - h * width
    place = jnp.where(((group >> 1) & 7) == z, place, -1)
    column = iota((width, ROWS), 0)
    top = jnp.max(logits, axis=0, keepdims=True)
    total = jnp.sum(jnp.exp(logits - top), axis=0, keepdims=True)
    lines = [top, total, jnp.zeros((6, ROWS), F32)]
    for k in range(TOP):
        lines.append(
            jnp.sum(jnp.where(column == place[k : k + 1, :], logits, 0.0), axis=0, keepdims=True)
        )
    lines = jnp.concatenate(lines, axis=0)
    for d in range(HID):
        out_ref[d, 0] = lines


def finish_kernel(at_ref, fine_ref, coarse_ref, routes_ref, loss_ref, prob_ref):
    core = at_ref[2]
    routes = routes_ref[...]
    groups = HID * NX * NZ
    index = iota((groups, ROWS), 0)
    upper = strict_upper()
    chip = ((index >> 3) & 3) * (NZ * NC) + (index & 7) * NC
    packed = fine_ref[...]
    masses, hits, ids = [], [], []
    target = jnp.zeros((1, ROWS), F32)
    for b in range(QB // HID):
        q = (index >> 5) * (QB // HID) + b
        block = (chip + other(core, q >> 3)) * BLK + (q & 7)
        hit = jnp.zeros((groups, ROWS), F32)
        for k in range(TOP):
            hit = jnp.where(routes[k : k + 1, :] == block, 1.0, hit)
        rank = dot(hit.astype(BF16), upper)
        slot = jnp.where(hit > 0.5, rank, -1.0)
        mass = jnp.zeros((groups, ROWS), F32)
        value = jnp.zeros((groups, ROWS), F32)
        for r in range(CAP):
            here = slot == float(r)
            mass = jnp.where(here, packed[:, r * 8 + b : r * 8 + b + 1], mass)
            value = jnp.where(here, packed[:, r * 8 + 4 + b : r * 8 + 5 + b], value)
        target = target + jnp.sum(value, axis=0, keepdims=True)
        masses.append(mass)
        ids.append(block)
    pair = []
    for k in range(TOP):
        line = jnp.zeros((1, ROWS), F32)
        for b in range(QB // HID):
            line = line + jnp.sum(
                jnp.where(routes[k : k + 1, :] == ids[b], masses[b], 0.0), axis=0, keepdims=True
            )
        pair.append(line)
    pair = jnp.concatenate(pair, axis=0)
    top = jnp.max(pair, axis=0, keepdims=True)
    fine_lse = top + jnp.log(jnp.sum(jnp.exp(pair - top), axis=0, keepdims=True))
    log_prob = pair - fine_lse
    prob = jnp.exp(log_prob)

    parts = coarse_ref[...]
    tops = parts[:, 0, :]
    peak = jnp.max(tops, axis=0, keepdims=True)
    total = jnp.sum(parts[:, 1, :] * jnp.exp(tops - peak), axis=0, keepdims=True)
    coarse_lse = peak + jnp.log(total)
    picked = jnp.sum(parts[:, 8:16, :], axis=0) - coarse_lse
    kl = jnp.sum(prob * (log_prob - picked), axis=0, keepdims=True)
    loss_ref[...] = fine_lse - target + kl
    prob_ref[...] = prob


def params(**more):
    return pltpu.CompilerParams(vmem_limit_bytes=VMEM, **more)


def smem():
    return pl.BlockSpec(memory_space=pltpu.SMEM)


def local(features, coarse_weight, fine_weight, block_cluster, routes, target_route, target_offset):
    ax = lax.axis_index
    at = jnp.stack([ax("x"), ax("z"), ax("c"), ax("hid")]).astype(I32)
    routes_t = routes.T
    place = jnp.concatenate(
        [target_route[None], target_offset[None], jnp.zeros((TOP - 2, ROWS), I32)], axis=0
    )
    table = jnp.concatenate(
        [block_cluster[None] // 64, block_cluster[None] % 64, jnp.zeros((14, block_cluster.shape[0]), I32)],
        axis=0,
    ).astype(BF16)

    peer_weight = lax.ppermute(fine_weight, "c", [(0, 1), (1, 0)])
    coarse_t = jnp.broadcast_to(coarse_weight.T[None], (NX * NC, coarse_weight.shape[1], PART))
    coarse_t = lax.all_to_all(coarse_t, ("x", "c"), 0, 0, tiled=True)
    coarse_t = coarse_t.reshape(-1, PART)
    columns = coarse_t.shape[0]

    packed = pl.pallas_call(
        pack_kernel,
        out_shape=jax.ShapeDtypeStruct((EXT, PART), BF16),
        compiler_params=params(),
    )(features, routes_t, place, table)
    gathered = lax.all_gather(packed, "z", axis=0, tiled=False)

    rows, coarse, offsets = pl.pallas_call(
        select_kernel,
        grid=(NZ // 2,),
        in_specs=[
            smem(),
            pl.BlockSpec((2, EXT, PART), lambda j: (j, 0, 0)),
            pl.BlockSpec((columns, PART), lambda j: (0, 0)),
        ],
        out_specs=[
            pl.BlockSpec((NX, QB, 2 * CAP, PART), lambda j: (0, 0, j, 0)),
            pl.BlockSpec((columns, 2 * ROWS), lambda j: (0, j)),
            pl.BlockSpec((NX * QB, ROWS), lambda j: (0, 0)),
        ],
        out_shape=[
            jax.ShapeDtypeStruct((NX, QB, NZ * CAP, PART), BF16),
            jax.ShapeDtypeStruct((columns, NZ * ROWS), F32),
            jax.ShapeDtypeStruct((NX * QB, ROWS), F32),
        ],
        compiler_params=params(),
    )(at, gathered, coarse_t)

    coarse = lax.psum_scatter(coarse, "hid", scatter_dimension=0, tiled=True)
    got_offsets = lax.all_to_all(offsets.reshape(NX, QB, ROWS), "x", 0, 0, tiled=True)
    got_rows = lax.all_to_all(rows, "x", 0, 0, tiled=True)

    coarse_lines = pl.pallas_call(
        coarse_kernel,
        grid=(NZ,),
        in_specs=[
            smem(),
            pl.BlockSpec((columns // HID, ROWS), lambda j: (0, j)),
            pl.BlockSpec((1, INFO, PART), lambda j: (j, ROWS // INFO, 0)),
        ],
        out_specs=pl.BlockSpec((HID, 1, 16, ROWS), lambda j: (0, j, 0, 0)),
        out_shape=jax.ShapeDtypeStruct((HID, NZ, 16, ROWS), F32),
        compiler_params=params(),
    )(at, coarse, gathered)
    coarse_lines = lax.all_to_all(
        coarse_lines.reshape(HID * NZ, 16, ROWS), ("hid", "z"), 0, 0, tiled=True
    )

    slots = NX * NZ * CAP
    fine = pl.pallas_call(
        fine_kernel,
        grid=(QB,),
        in_specs=[
            pl.BlockSpec((NX, 1, NZ * CAP, PART), lambda b: (0, b, 0, 0)),
            pl.BlockSpec((1, PART, LBL), lambda b: (jnp.minimum(b, BLK - 1), 0, 0)),
            pl.BlockSpec((1, PART, LBL), lambda b: (jnp.maximum(b - BLK, 0), 0, 0)),
        ],
        out_specs=pl.BlockSpec((1, slots, LBL), lambda b: (b, 0, 0)),
        out_shape=jax.ShapeDtypeStruct((QB, slots, LBL), F32),
        compiler_params=params(),
    )(got_rows, fine_weight, peer_weight)
    fine = lax.psum_scatter(fine, "hid", scatter_dimension=0, tiled=True)

    whole = pl.BlockSpec(memory_space=pltpu.VMEM)
    scores = pl.pallas_call(
        score_kernel,
        in_specs=[smem(), whole, whole],
        out_specs=whole,
        out_shape=jax.ShapeDtypeStruct((HID, NX * NZ, 128), F32),
        compiler_params=params(),
    )(at, fine, got_offsets)
    scores = lax.all_to_all(
        scores.reshape(HID * NX * NZ, 128), ("hid", "x", "z"), 0, 0, tiled=True
    )

    loss, prob = pl.pallas_call(
        finish_kernel,
        in_specs=[smem(), whole, whole, whole],
        out_specs=[whole, whole],
        out_shape=[jax.ShapeDtypeStruct((1, ROWS), F32), jax.ShapeDtypeStruct((TOP, ROWS), F32)],
        compiler_params=params(),
    )(at, scores, coarse_lines, routes_t)
    return loss.reshape(ROWS), prob.T


def solution(mesh):
    fine_mesh = Mesh(mesh.devices.reshape(HID, NX, NZ, NC), ("hid", "x", "z", "c"))
    blk = ("x", "z", "c")
    placed = (P(blk, "hid"), P("hid", blk), P(blk, "hid", None), P(), P(blk, None), P(blk), P(blk))
    return jax.shard_map(
        local, mesh=fine_mesh, in_specs=placed, out_specs=(P(blk), P(blk, None)), check_vma=False
    )
```

```python
import jax
import jax.numpy as jnp
from jax import lax
from jax.experimental import pallas as pl
from jax.experimental.pallas import tpu as pltpu
from jax.sharding import Mesh, PartitionSpec as P

F32 = jnp.float32
BF16 = jnp.bfloat16
I32 = jnp.int32

HID, NX, NZ, NC = 4, 4, 8, 2
ROWS = 256
PART = 1024
TOP = 8
BLK = 8
QB = NC * BLK
CAP = 8
LBL = 256
INFO = 16
SLOTS = 48
TIERS = SLOTS // CAP
PAIR = 2 * CAP
WIDE = 2 * ROWS
AWAY = ((0, 1, -1, 2), (-2, 3, -3, 4))
FOUR = 2 * PAIR
ARRIVE = {0: range(0, 2), 2: range(2, BLK), BLK: range(BLK, QB)}
GROUPS = NC * NX
EXT = ROWS + INFO
VMEM = 56 * 1024 * 1024


def iota(shape, dim):
    return lax.broadcasted_iota(I32, shape, dim)


def dot(a, b):
    return jnp.dot(a, b, preferred_element_type=F32)


def strict_upper():
    return jnp.where(iota((ROWS, ROWS), 0) < iota((ROWS, ROWS), 1), 1.0, 0.0).astype(BF16)


def other(core, half):
    return core + half - 2 * core * half


def pack_kernel(f_ref, routes_ref, place_ref, offset_ref, cluster_ref, out_ref):
    out_ref[0:ROWS, :] = f_ref[...]
    routes = routes_ref[...]
    clusters = cluster_ref[...]
    count = clusters.shape[1]
    table = jnp.concatenate([clusters >> 6, clusters & 63, jnp.zeros((14, count), I32)], axis=0)
    table = table.astype(F32).astype(BF16)
    groups, columns = [], []
    blocks = iota((count, ROWS), 0)
    for k in range(TOP):
        hot = jnp.where(blocks == routes[k : k + 1, :], 1.0, 0.0).astype(BF16)
        found = dot(table, hot)
        groups.append(found[0:1, :])
        columns.append(found[1:2, :])
    places = [place_ref[...].astype(F32), offset_ref[...].astype(F32), jnp.zeros((6, ROWS), F32)]
    left = jnp.concatenate([(routes - 256).astype(F32)] + columns, axis=0)
    right = jnp.concatenate(groups + places, axis=0)
    rest = jnp.zeros((INFO, PART - WIDE), F32)
    out_ref[ROWS:EXT, :] = jnp.concatenate([left, right, rest], axis=1).astype(BF16)


def select_more_kernel(at_ref, a_ref, b_ref, begun_ref, rows_ref):
    select_kernel(at_ref, a_ref, b_ref, rows_ref)


def select_kernel(at_ref, a_ref, b_ref, rows_ref):
    z, core = at_ref[1], at_ref[2]
    count = GROUPS * BLK
    index = iota((count, ROWS), 0)
    device = ((index >> 3) & 3) * (NZ * NC) + z * NC + other(core, index >> 5)
    blocks = device * BLK + (index & 7)
    upper = strict_upper()
    ones = jnp.ones((ROWS, ROWS), BF16)
    row, col = iota((count, count), 0), iota((count, count), 1)
    before = jnp.where(((row >> 3) == (col >> 3)) & (col < row), 1.0, 0.0).astype(BF16)
    slot_of = iota((SLOTS, ROWS), 0).astype(F32)
    eye = iota((SLOTS, 128), 0) == iota((SLOTS, 128), 1)

    def as_line(column):
        return jnp.sum(jnp.where(eye, column, 0.0), axis=0, keepdims=True)

    picked, owners, places = [], [], []
    for g_ref in (a_ref, b_ref):
        info = g_ref[ROWS:EXT, 0:WIDE].astype(F32)
        routes = info[0:TOP, 0:ROWS].astype(I32) + 256
        place = info[TOP : TOP + 1, ROWS:].astype(I32)
        offset = info[TOP + 1 : TOP + 2, ROWS:]
        hit = jnp.zeros((count, ROWS), F32)
        target = jnp.zeros((1, ROWS), I32)
        for k in range(TOP):
            hit = jnp.where(routes[k : k + 1, :] == blocks, 1.0, hit)
            target = jnp.where(place == k, routes[k : k + 1, :], target)
        held = hit.astype(BF16)
        start = dot(before, dot(held, ones).astype(BF16))
        slot = jnp.where(hit > 0.5, dot(held, upper) + start, -1.0)
        wanted = jnp.where(blocks == target, slot, -1.0)
        hots = []
        for g in range(GROUPS):
            label = jnp.full((SLOTS, ROWS), -1.0, F32)
            for b in range(BLK):
                label = jnp.where(slot[g * BLK + b : g * BLK + b + 1, :] == slot_of, float(b), label)
            hots.append(jnp.where(label > -0.5, 1.0, 0.0).astype(BF16))
            owners.append(as_line(jnp.max(label, axis=1, keepdims=True)))
            mine = jnp.max(wanted[g * BLK : (g + 1) * BLK, :], axis=0, keepdims=True)
            places.append(
                as_line(
                    jnp.sum(jnp.where(mine == slot_of, offset + 1.0, 0.0), axis=1, keepdims=True)
                )
            )
        hots = jnp.concatenate(hots, axis=0)
        picked.append(dot(hots, g_ref[0:ROWS, :]).reshape(GROUPS, TIERS, CAP, PART))
    both = jnp.concatenate(picked, axis=2).astype(BF16)
    for g in range(GROUPS):
        rows_ref[g % NX, (g // NX) * TIERS : (g // NX + 1) * TIERS] = both[g]
    for d in range(NX):
        lines = []
        for half in range(NC):
            g = half * NX + d
            lines += [owners[g], owners[GROUPS + g], places[g], places[GROUPS + g]]
        lines = jnp.concatenate(lines + [jnp.zeros((8, 128), F32)], axis=0)
        lines = jnp.concatenate([lines, jnp.zeros((PAIR, PART - 128), F32)], axis=1)
        rows_ref[d, NC * TIERS] = lines.astype(BF16)


def partial_kernel(a_ref, b_ref, c_ref, d_ref, w_ref, out_ref):
    for s, ref in enumerate((a_ref, b_ref, c_ref, d_ref)):
        out_ref[:, s * ROWS : (s + 1) * ROWS] = lax.dot_general(
            w_ref[...], ref[0:ROWS, :], (((1,), (1,)), ((), ())), preferred_element_type=F32
        )


def slot_lines(meta, half, kind):
    eye = iota((SLOTS, 128), 0) == iota((SLOTS, 128), 1)
    columns = []
    for s in range(4):
        at = (s // 2) * PAIR + half * 4 + kind * 2 + s % 2
        column = jnp.sum(jnp.where(eye, meta[at : at + 1, :], 0.0), axis=1, keepdims=True)
        columns.append(jnp.broadcast_to(column, (SLOTS, LBL)))
    return jnp.concatenate(
        [c[t * CAP : (t + 1) * CAP, :] for t in range(TIERS) for c in columns], axis=0
    )


def fine_kernel(own_ref, peer_ref, r_ref, out_ref, held_ref, owner_ref, sems):
    copies = []
    for i in range(QB):
        source = own_ref if i < BLK else peer_ref
        copies.append(pltpu.make_async_copy(source.at[i % BLK], held_ref.at[i], sems.at[i]))
        copies[i].start()
    for half in range(NC):
        for x in range(NX):
            meta = r_ref[x, NC * TIERS, :, 0:128].astype(F32)
            owner_ref[x] = slot_lines(meta, half, 0).reshape(TIERS, FOUR, LBL)
        for b in range(BLK):
            for i in ARRIVE.get(half * BLK + b, ()):
                copies[i].wait()
            end = min(b + 1, TIERS)
            rows = r_ref[:, half * TIERS : half * TIERS + end].reshape(NX * end * FOUR, PART)
            part = dot(rows, held_ref[half * BLK + b])
            for x in range(NX):
                for t in range(end):
                    at = (x * end + t) * FOUR
                    piece = part[at : at + FOUR]
                    if t < b:
                        piece = jnp.where(owner_ref[x, t] == float(b), piece, out_ref[x, half, t])
                    out_ref[x, half, t] = piece


def score(y, h, meta_ref):
    rows = NC * TIERS * FOUR
    y = y.reshape(rows, LBL)
    meta = meta_ref[h, 0, :, 0:128].astype(F32)
    wanted = jnp.concatenate([slot_lines(meta, half, 1) for half in range(NC)], axis=0)
    label = iota((rows, LBL), 1).astype(F32) + 1.0
    top = jnp.max(y, axis=1, keepdims=True)
    mass = top + jnp.log(jnp.sum(jnp.exp(y - top), axis=1, keepdims=True))
    target = jnp.sum(jnp.where(label == wanted, y, 0.0), axis=1, keepdims=True)
    order = iota((rows, LBL), 0)
    tier = order // FOUR
    half = jnp.where(tier >= TIERS, 1, 0)
    slot = half * 128 + (tier - half * TIERS) * CAP + (order & 7)
    lane = iota((rows, LBL), 1)
    packed = jnp.where(lane == slot, mass, 0.0) + jnp.where(lane == slot + 64, target, 0.0)
    packed = jnp.sum(packed.reshape(NC * TIERS, 4, CAP, LBL), axis=2)
    return jnp.sum(packed, axis=0)


def score_kernel(at_ref, y_ref, meta_ref, out_ref):
    out_ref[0:4, :] = score(y_ref[0], at_ref[3], meta_ref)
    out_ref[4:8, :] = jnp.zeros((4, LBL), F32)


def score_last_kernel(at_ref, y_ref, meta_ref, first_ref, out_ref):
    z, core, h = at_ref[1], at_ref[2], at_ref[3]
    y = y_ref[0] + y_ref[1] + y_ref[2] + y_ref[3]
    last = score(y, h, meta_ref)
    out_ref[...] = jnp.zeros_like(out_ref)
    for i, lines in enumerate((first_ref, last)):
        for s in range(4):
            to = (z + NZ + AWAY[i][s]) & (NZ - 1)
            for d in range(HID):
                at = (((d * NX + h) * NZ + to) * NC + core) * NC
                for half in range(NC):
                    line = lines[s : s + 1, half * 128 : (half + 1) * 128]
                    out_ref[pl.ds(at + half, 1), :] = line


def coarse_lines(at_ref, c_ref, infos):
    z, h = at_ref[1], at_ref[3]
    width = c_ref.shape[0]
    column = iota((width, ROWS), 0)
    out = []
    for s, info_ref in enumerate(infos):
        logits = c_ref[:, s * ROWS : (s + 1) * ROWS]
        info = info_ref[...].astype(F32).astype(I32)
        inside = info[TOP : 2 * TOP, 0:ROWS]
        group = info[0:TOP, ROWS:WIDE]
        place = ((group >> 4) * NC + (group & 1)) * 64 + inside - h * width
        place = jnp.where(((group >> 1) & 7) == z, place, -1)
        top = jnp.max(logits, axis=0, keepdims=True)
        total = jnp.sum(jnp.exp(logits - top), axis=0, keepdims=True)
        lines = [top, total, jnp.zeros((6, ROWS), F32)]
        for k in range(TOP):
            lines.append(
                jnp.sum(
                    jnp.where(column == place[k : k + 1, :], logits, 0.0), axis=0, keepdims=True
                )
            )
        out.append(jnp.concatenate(lines, axis=0))
    return out


def coarse_kernel(at_ref, c_ref, i0, i1, i2, i3, out_ref):
    for s, lines in enumerate(coarse_lines(at_ref, c_ref, (i0, i1, i2, i3))):
        out_ref[s] = lines


def coarse_last_kernel(at_ref, c_ref, i0, i1, i2, i3, first_ref, out_ref):
    z = at_ref[1]
    last = coarse_lines(at_ref, c_ref, (i0, i1, i2, i3))
    away = [d for four in AWAY for d in four]
    for i in range(NZ):
        lines = first_ref[i] if i < NZ // 2 else last[i - NZ // 2]
        for d in range(HID):
            out_ref[d, (z + NZ + away[i]) & (NZ - 1)] = lines


def finish_kernel(at_ref, fine_ref, coarse_ref, routes_ref, loss_ref, prob_ref):
    x, core = at_ref[0], at_ref[2]
    routes = routes_ref[...]
    chips = NX * NZ
    index = iota((QB * chips, ROWS), 0)
    q = index >> 5
    block = ((index & 31) * NC + other(core, q >> 3)) * BLK + (q & 7)
    hit = jnp.zeros((QB * chips, ROWS), F32)
    for k in range(TOP):
        hit = jnp.where(routes[k : k + 1, :] == block, 1.0, hit)
    held = hit.astype(BF16)
    rank = dot(held, strict_upper())
    count = dot(held, jnp.ones((ROWS, ROWS), BF16))
    slots = []
    for half in range(NC):
        start = jnp.zeros((chips, ROWS), F32)
        for b in range(BLK):
            at = (half * BLK + b) * chips
            slots.append(rank[at : at + chips] + start)
            start = start + count[at : at + chips]
    slots = jnp.concatenate(slots, axis=0)

    table = fine_ref[pl.ds(x * (chips * NC * NC), chips * NC * NC), :]
    high = table.astype(BF16)
    rest = table - high.astype(F32)
    middle = rest.astype(BF16)
    low = (rest - middle.astype(F32)).astype(BF16)
    pieces = jnp.concatenate([high, middle, low], axis=0)
    row_of = iota((chips * NC * NC, ROWS), 0)
    lane_of = iota((128, ROWS), 0).astype(F32)
    pair = []
    target = jnp.zeros((1, ROWS), F32)
    for k in range(TOP):
        route = routes[k : k + 1, :]
        slot = jnp.sum(jnp.where(route == block, slots, 0.0), axis=0, keepdims=True)
        line = ((route >> 4) * NC + core) * NC + other(core, (route >> 3) & 1)
        hot = jnp.where(line == row_of, 1.0, 0.0).astype(BF16)
        found = lax.dot_general(
            pieces,
            jnp.concatenate([hot, hot, hot], axis=0),
            (((0,), (0,)), ((), ())),
            preferred_element_type=F32,
        )
        pair.append(jnp.sum(jnp.where(lane_of == slot, found, 0.0), axis=0, keepdims=True))
        target = target + jnp.sum(
            jnp.where(lane_of == slot + 64.0, found, 0.0), axis=0, keepdims=True
        )
    pair = jnp.concatenate(pair, axis=0)
    top = jnp.max(pair, axis=0, keepdims=True)
    fine_lse = top + jnp.log(jnp.sum(jnp.exp(pair - top), axis=0, keepdims=True))
    log_prob = pair - fine_lse
    prob = jnp.exp(log_prob)

    parts = coarse_ref[...]
    tops = parts[:, 0, :]
    peak = jnp.max(tops, axis=0, keepdims=True)
    total = jnp.sum(parts[:, 1, :] * jnp.exp(tops - peak), axis=0, keepdims=True)
    coarse_lse = peak + jnp.log(total)
    picked = jnp.sum(parts[:, 8:16, :], axis=0) - coarse_lse
    kl = jnp.sum(prob * (log_prob - picked), axis=0, keepdims=True)
    loss_ref[...] = fine_lse - target + kl
    prob_ref[...] = prob


def params(**more):
    return pltpu.CompilerParams(vmem_limit_bytes=VMEM, **more)


def smem():
    return pl.BlockSpec(memory_space=pltpu.SMEM)


def shape(dims, kind):
    return jax.ShapeDtypeStruct(dims, kind)


def swap(value, axes, split=0):
    return lax.all_to_all(value, axes, split, split, tiled=True)


def local(features, coarse_weight, fine_weight, block_cluster, routes, target_route, target_offset):
    ax = lax.axis_index
    at = jnp.stack([ax("x"), ax("z"), ax("c"), ax("hid")]).astype(I32)
    hbm = pl.BlockSpec(memory_space=pl.ANY)
    routes_t = routes.T

    full = lambda *dims: pl.BlockSpec(dims, lambda i: (0,) * len(dims))

    def run(kernel, specs, out, *operands, out_specs=None, scratch=(), **more):
        outs = out if isinstance(out, list) else [out]
        specs = [full(*o.shape) if spec is None else spec for spec, o in zip(specs, operands)]
        return pl.pallas_call(
            kernel,
            grid=(1,),
            in_specs=specs,
            out_specs=out_specs or [full(*o.shape) for o in outs],
            out_shape=outs,
            scratch_shapes=scratch,
            compiler_params=params(),
            **more,
        )(*operands)

    (here,) = run(
        pack_kernel,
        [None] * 5,
        shape((EXT, PART), BF16),
        features,
        routes_t,
        target_route[None],
        target_offset[None],
        block_cluster[None],
    )
    up = [(i, (i + 1) % NZ) for i in range(NZ)]
    down = [(i, (i - 1) % NZ) for i in range(NZ)]
    from_up, from_down = [here], [here]
    for step in range(NZ // 2):
        if step < NZ // 2 - 1:
            from_up.append(lax.ppermute(from_up[-1], "z", down))
        from_down.append(lax.ppermute(from_down[-1], "z", up))
    peer_weight = lax.ppermute(fine_weight, "c", [(0, 1), (1, 0)])
    coarse_t = lax.all_gather(coarse_weight.T, ("x", "c"), axis=0, tiled=True)
    columns = coarse_t.shape[0]

    near = (here, from_up[1], from_down[1], from_up[2])
    far = (from_down[2], from_up[3], from_down[3], from_down[4])
    tiers = NC * TIERS + 1
    last_run = [here]

    def in_turn(call, first, *more):
        first, _ = lax.optimization_barrier((first, last_run[0]))
        (last_run[0],) = call(first, *more)
        return last_run[0]

    def select(four, *waits):
        out = shape((NX, tiers, FOUR, PART), BF16)
        block = (NX, tiers, PAIR, PART)

        def begin(a, b):
            to = pl.BlockSpec(block, lambda i: (0, 0, 0, 0))
            return run(select_kernel, [smem(), None, None], out, at, a, b, out_specs=[to])

        def end(a, b, begun):
            to = pl.BlockSpec(block, lambda i: (0, 0, 1, 0))
            specs = [smem(), None, None, hbm]
            return run(
                select_more_kernel,
                specs,
                out,
                at,
                a,
                b,
                begun,
                out_specs=[to],
                input_output_aliases={3: 0},
            )

        first = lax.optimization_barrier((four[0], waits[0]))[0]
        begun = in_turn(begin, first, four[1])
        first = lax.optimization_barrier((four[2], waits[1]))[0]
        return swap(in_turn(end, first, four[3], begun), "x")

    def partial(four, *waits):
        def call(*four):
            out = shape((columns, NX * ROWS), F32)
            return run(partial_kernel, [None] * 5, out, *four, coarse_t)

        first = lax.optimization_barrier((four[0], *waits))[0]
        out = in_turn(call, first, *four[1:])
        return lax.psum_scatter(out, "hid", scatter_dimension=0, tiled=True)

    info = pl.BlockSpec((INFO, WIDE), lambda i: (ROWS // INFO, 0))

    def coarse(kernel, part, four, out, *more):
        def call(c):
            specs = [smem(), None] + [info] * 4 + [None] * len(more)
            return run(kernel, specs, out, at, c, *four, *more)

        return in_turn(call, part)

    def fine(rows):
        def call(rows):
            return run(
                fine_kernel,
                [hbm, hbm, None],
                shape((NX, NC, TIERS, FOUR, LBL), F32),
                fine_weight,
                peer_weight,
                rows,
                scratch=[
                    pltpu.VMEM((QB, PART, LBL), BF16),
                    pltpu.VMEM((NX, TIERS, FOUR, LBL), F32),
                    pltpu.SemaphoreType.DMA((QB,)),
                ],
                cost_estimate=pl.CostEstimate(
                    flops=8 * 10**9, bytes_accessed=40 * 2**20, transcendentals=0
                ),
            )

        return in_turn(call, rows)

    meta = pl.BlockSpec((NX, 1, FOUR, PART), lambda i: (0, NC * TIERS, 0, 0))

    def scored(kernel, fine, rows, out, *before):
        def call(fine):
            specs = [smem(), None, meta] + [None] * len(before)
            return run(kernel, specs, out, at, fine, rows, *before)

        return in_turn(call, fine)

    rows_near = select(near, from_down[1], from_down[2])
    part_near = partial(near)
    rows_far = select(far, from_down[3], from_down[4])
    part_far = partial(far, rows_near)
    fine_near = lax.psum_scatter(fine(rows_near), "hid", scatter_dimension=0, tiled=True)
    lines = coarse(coarse_kernel, part_near, near, shape((NZ // 2, 16, ROWS), F32))
    lines = coarse(coarse_last_kernel, part_far, far, shape((HID, NZ, 16, ROWS), F32), lines)
    lines = swap(lines.reshape(HID * NZ, 16, ROWS), ("hid", "z"))
    fine_far, lines = lax.optimization_barrier((fine(rows_far), lines))
    fine_far = swap(fine_far, "hid")
    first = scored(score_kernel, fine_near, rows_near, shape((8, LBL), F32))
    table = scored(
        score_last_kernel, fine_far, rows_far, shape((HID * NX * NZ * NC * NC, 128), F32), first
    )
    table = swap(table, ("hid", "x", "z", "c"))

    loss, prob = run(
        finish_kernel,
        [smem(), None, None, None],
        [shape((1, ROWS), F32), shape((TOP, ROWS), F32)],
        at,
        table,
        lines,
        routes_t,
    )
    return loss.reshape(ROWS), prob.T


def solution(mesh):
    fine_mesh = Mesh(mesh.devices.reshape(HID, NX, NZ, NC), ("hid", "x", "z", "c"))
    blk = ("x", "z", "c")
    placed = (P(blk, "hid"), P("hid", blk), P(blk, "hid", None), P(), P(blk, None), P(blk), P(blk))
    return jax.shard_map(
        local, mesh=fine_mesh, in_specs=placed, out_specs=(P(blk), P(blk, None)), check_vma=False
    )
```

```python
import jax
import jax.numpy as jnp
from jax import lax
from jax.experimental import pallas as pl
from jax.experimental.pallas import tpu as pltpu
from jax.sharding import Mesh, PartitionSpec as P

F32 = jnp.float32
BF16 = jnp.bfloat16
I32 = jnp.int32

HID, NX, NZ, NC = 4, 4, 8, 2
ROWS = 256
PART = 1024
TOP = 8
BLK = 8
QB = NC * BLK
CAP = 8
LBL = 256
INFO = 16
SLOTS = 48
TIERS = SLOTS // CAP
PAIR = 2 * CAP
WIDE = 2 * ROWS
AWAY = ((0, 1, -1, 2), (-2, 3, -3, 4))
FOUR = 2 * PAIR
ARRIVE = {0: range(0, 2), 2: range(2, BLK), BLK: range(BLK, QB)}
GROUPS = NC * NX
EXT = ROWS + INFO
VMEM = 56 * 1024 * 1024


def iota(shape, dim):
    return lax.broadcasted_iota(I32, shape, dim)


def dot(a, b):
    return jnp.dot(a, b, preferred_element_type=F32)


def strict_upper():
    return jnp.where(iota((ROWS, ROWS), 0) < iota((ROWS, ROWS), 1), 1.0, 0.0).astype(BF16)


def other(core, half):
    return core + half - 2 * core * half


def pack_kernel(f_ref, routes_ref, place_ref, offset_ref, cluster_ref, out_ref):
    out_ref[0:ROWS, :] = f_ref[...]
    routes = routes_ref[...]
    clusters = cluster_ref[...]
    count = clusters.shape[1]
    table = jnp.concatenate([clusters >> 6, clusters & 63, jnp.zeros((14, count), I32)], axis=0)
    table = table.astype(F32).astype(BF16)
    groups, columns = [], []
    blocks = iota((count, ROWS), 0)
    for k in range(TOP):
        hot = jnp.where(blocks == routes[k : k + 1, :], 1.0, 0.0).astype(BF16)
        found = dot(table, hot)
        groups.append(found[0:1, :])
        columns.append(found[1:2, :])
    places = [place_ref[...].astype(F32), offset_ref[...].astype(F32), jnp.zeros((6, ROWS), F32)]
    left = jnp.concatenate([(routes - 256).astype(F32)] + columns, axis=0)
    right = jnp.concatenate(groups + places, axis=0)
    rest = jnp.zeros((INFO, PART - WIDE), F32)
    out_ref[ROWS:EXT, :] = jnp.concatenate([left, right, rest], axis=1).astype(BF16)


def select_more_kernel(at_ref, a_ref, b_ref, begun_ref, rows_ref):
    select_kernel(at_ref, a_ref, b_ref, rows_ref)


def select_kernel(at_ref, a_ref, b_ref, rows_ref):
    z, core = at_ref[1], at_ref[2]
    count = GROUPS * BLK
    index = iota((count, ROWS), 0)
    device = ((index >> 3) & 3) * (NZ * NC) + z * NC + other(core, index >> 5)
    blocks = device * BLK + (index & 7)
    upper = strict_upper()
    ones = jnp.ones((ROWS, ROWS), BF16)
    row, col = iota((count, count), 0), iota((count, count), 1)
    before = jnp.where(((row >> 3) == (col >> 3)) & (col < row), 1.0, 0.0).astype(BF16)
    slot_of = iota((SLOTS, ROWS), 0).astype(F32)
    eye = iota((SLOTS, 128), 0) == iota((SLOTS, 128), 1)

    def as_line(column):
        return jnp.sum(jnp.where(eye, column, 0.0), axis=0, keepdims=True)

    picked, owners, places = [], [], []
    for g_ref in (a_ref, b_ref):
        info = g_ref[ROWS:EXT, 0:WIDE].astype(F32)
        routes = info[0:TOP, 0:ROWS].astype(I32) + 256
        place = info[TOP : TOP + 1, ROWS:].astype(I32)
        offset = info[TOP + 1 : TOP + 2, ROWS:]
        hit = jnp.zeros((count, ROWS), F32)
        target = jnp.zeros((1, ROWS), I32)
        for k in range(TOP):
            hit = jnp.where(routes[k : k + 1, :] == blocks, 1.0, hit)
            target = jnp.where(place == k, routes[k : k + 1, :], target)
        held = hit.astype(BF16)
        start = dot(before, dot(held, ones).astype(BF16))
        slot = jnp.where(hit > 0.5, dot(held, upper) + start, -1.0)
        wanted = jnp.where(blocks == target, slot, -1.0)
        hots = []
        for g in range(GROUPS):
            label = jnp.full((SLOTS, ROWS), -1.0, F32)
            for b in range(BLK):
                label = jnp.where(slot[g * BLK + b : g * BLK + b + 1, :] == slot_of, float(b), label)
            hots.append(jnp.where(label > -0.5, 1.0, 0.0).astype(BF16))
            owners.append(as_line(jnp.max(label, axis=1, keepdims=True)))
            mine = jnp.max(wanted[g * BLK : (g + 1) * BLK, :], axis=0, keepdims=True)
            places.append(
                as_line(
                    jnp.sum(jnp.where(mine == slot_of, offset + 1.0, 0.0), axis=1, keepdims=True)
                )
            )
        hots = jnp.concatenate(hots, axis=0)
        picked.append(dot(hots, g_ref[0:ROWS, :]).reshape(GROUPS, TIERS, CAP, PART))
    both = jnp.concatenate(picked, axis=2).astype(BF16)
    for g in range(GROUPS):
        rows_ref[g % NX, (g // NX) * TIERS : (g // NX + 1) * TIERS] = both[g]
    for d in range(NX):
        lines = []
        for half in range(NC):
            g = half * NX + d
            lines += [owners[g], owners[GROUPS + g], places[g], places[GROUPS + g]]
        lines = jnp.concatenate(lines + [jnp.zeros((8, 128), F32)], axis=0)
        lines = jnp.concatenate([lines, jnp.zeros((PAIR, PART - 128), F32)], axis=1)
        rows_ref[d, NC * TIERS] = lines.astype(BF16)


def partial_kernel(a_ref, b_ref, c_ref, d_ref, w_ref, out_ref):
    for s, ref in enumerate((a_ref, b_ref, c_ref, d_ref)):
        out_ref[:, s * ROWS : (s + 1) * ROWS] = lax.dot_general(
            w_ref[...], ref[0:ROWS, :], (((1,), (1,)), ((), ())), preferred_element_type=F32
        )


def slot_lines(meta, half, kind):
    eye = iota((SLOTS, 128), 0) == iota((SLOTS, 128), 1)
    columns = []
    for s in range(4):
        at = (s // 2) * PAIR + half * 4 + kind * 2 + s % 2
        column = jnp.sum(jnp.where(eye, meta[at : at + 1, :], 0.0), axis=1, keepdims=True)
        columns.append(jnp.broadcast_to(column, (SLOTS, LBL)))
    return jnp.concatenate(
        [c[t * CAP : (t + 1) * CAP, :] for t in range(TIERS) for c in columns], axis=0
    )


def fine_kernel(own_ref, peer_ref, r_ref, out_ref, held_ref, owner_ref, sems):
    copies = []
    for i in range(QB):
        source = own_ref if i < BLK else peer_ref
        copies.append(pltpu.make_async_copy(source.at[i % BLK], held_ref.at[i], sems.at[i]))
        copies[i].start()
    for half in range(NC):
        for x in range(NX):
            meta = r_ref[x, NC * TIERS, :, 0:128].astype(F32)
            owner_ref[x] = slot_lines(meta, half, 0).reshape(TIERS, FOUR, LBL)
        for b in range(BLK):
            for i in ARRIVE.get(half * BLK + b, ()):
                copies[i].wait()
            end = min(b + 1, TIERS)
            rows = r_ref[:, half * TIERS : half * TIERS + end].reshape(NX * end * FOUR, PART)
            part = dot(rows, held_ref[half * BLK + b])
            for x in range(NX):
                for t in range(end):
                    at = (x * end + t) * FOUR
                    piece = part[at : at + FOUR]
                    if t < b:
                        piece = jnp.where(owner_ref[x, t] == float(b), piece, out_ref[x, half, t])
                    out_ref[x, half, t] = piece


def score(y, h, meta_ref):
    rows = NC * TIERS * FOUR
    y = y.reshape(rows, LBL)
    meta = meta_ref[h, 0, :, 0:128].astype(F32)
    wanted = jnp.concatenate([slot_lines(meta, half, 1) for half in range(NC)], axis=0)
    label = iota((rows, LBL), 1).astype(F32) + 1.0
    top = jnp.max(y, axis=1, keepdims=True)
    mass = top + jnp.log(jnp.sum(jnp.exp(y - top), axis=1, keepdims=True))
    target = jnp.sum(jnp.where(label == wanted, y, 0.0), axis=1, keepdims=True)
    order = iota((rows, LBL), 0)
    tier = order // FOUR
    half = jnp.where(tier >= TIERS, 1, 0)
    slot = half * 128 + (tier - half * TIERS) * CAP + (order & 7)
    lane = iota((rows, LBL), 1)
    packed = jnp.where(lane == slot, mass, 0.0) + jnp.where(lane == slot + 64, target, 0.0)
    packed = jnp.sum(packed.reshape(NC * TIERS, 4, CAP, LBL), axis=2)
    return jnp.sum(packed, axis=0)


def score_kernel(at_ref, y_ref, meta_ref, out_ref):
    out_ref[0:4, :] = score(y_ref[0], at_ref[3], meta_ref)
    out_ref[4:8, :] = jnp.zeros((4, LBL), F32)


def score_last_kernel(at_ref, y_ref, meta_ref, first_ref, out_ref):
    z, core, h = at_ref[1], at_ref[2], at_ref[3]
    y = y_ref[0] + y_ref[1] + y_ref[2] + y_ref[3]
    last = score(y, h, meta_ref)
    out_ref[...] = jnp.zeros_like(out_ref)
    for i, lines in enumerate((first_ref, last)):
        for s in range(4):
            to = (z + NZ + AWAY[i][s]) & (NZ - 1)
            for d in range(HID):
                at = (((d * NX + h) * NZ + to) * NC + core) * NC
                for half in range(NC):
                    line = lines[s : s + 1, half * 128 : (half + 1) * 128]
                    out_ref[pl.ds(at + half, 1), :] = line


def coarse_lines(at_ref, c_ref, infos):
    z, h = at_ref[1], at_ref[3]
    width = c_ref.shape[0]
    column = iota((width, ROWS), 0)
    out = []
    for s, info_ref in enumerate(infos):
        logits = c_ref[:, s * ROWS : (s + 1) * ROWS]
        info = info_ref[...].astype(F32).astype(I32)
        inside = info[TOP : 2 * TOP, 0:ROWS]
        group = info[0:TOP, ROWS:WIDE]
        place = ((group >> 4) * NC + (group & 1)) * 64 + inside - h * width
        place = jnp.where(((group >> 1) & 7) == z, place, -1)
        top = jnp.max(logits, axis=0, keepdims=True)
        total = jnp.sum(jnp.exp(logits - top), axis=0, keepdims=True)
        lines = [top, total, jnp.zeros((6, ROWS), F32)]
        for k in range(TOP):
            lines.append(
                jnp.sum(
                    jnp.where(column == place[k : k + 1, :], logits, 0.0), axis=0, keepdims=True
                )
            )
        out.append(jnp.concatenate(lines, axis=0))
    return out


def coarse_kernel(at_ref, c_ref, i0, i1, i2, i3, out_ref):
    for s, lines in enumerate(coarse_lines(at_ref, c_ref, (i0, i1, i2, i3))):
        out_ref[s] = lines


def coarse_last_kernel(at_ref, c_ref, i0, i1, i2, i3, first_ref, out_ref):
    last = coarse_lines(at_ref, c_ref, (i0, i1, i2, i3))
    for i in range(NZ):
        out_ref[i] = first_ref[i] if i < NZ // 2 else last[i - NZ // 2]


def coarse_sum_kernel(at_ref, own_ref, next_ref, across_ref, before_ref, out_ref):
    z = at_ref[1]
    away = [d for four in AWAY for d in four]
    out_ref[...] = jnp.zeros_like(out_ref)
    for i in range(NZ):
        to = (z + NZ + away[i]) & (NZ - 1)
        shards = [ref[i] for ref in (own_ref, across_ref, next_ref, before_ref)]
        top = shards[0][0:1]
        for shard in shards[1:]:
            top = jnp.maximum(top, shard[0:1])
        sums = [shard[1:2] * jnp.exp(shard[0:1] - top) for shard in shards]
        out_ref[to, pl.ds(2 * z, 1), :] = top
        out_ref[to, pl.ds(2 * z + 1, 1), :] = (sums[0] + sums[1]) + (sums[2] + sums[3])
        picks = [shard[8:16] for shard in shards]
        out_ref[to, 16:24, :] = (picks[0] + picks[1]) + (picks[2] + picks[3])


def finish_kernel(at_ref, fine_ref, coarse_ref, routes_ref, loss_ref, prob_ref):
    x, core = at_ref[0], at_ref[2]
    routes = routes_ref[...]
    chips = NX * NZ
    index = iota((QB * chips, ROWS), 0)
    q = index >> 5
    block = ((index & 31) * NC + other(core, q >> 3)) * BLK + (q & 7)
    hit = jnp.zeros((QB * chips, ROWS), F32)
    for k in range(TOP):
        hit = jnp.where(routes[k : k + 1, :] == block, 1.0, hit)
    held = hit.astype(BF16)
    rank = dot(held, strict_upper())
    count = dot(held, jnp.ones((ROWS, ROWS), BF16))
    slots = []
    for half in range(NC):
        start = jnp.zeros((chips, ROWS), F32)
        for b in range(BLK):
            at = (half * BLK + b) * chips
            slots.append(rank[at : at + chips] + start)
            start = start + count[at : at + chips]
    slots = jnp.concatenate(slots, axis=0)

    table = fine_ref[pl.ds(x * (chips * NC * NC), chips * NC * NC), :]
    high = table.astype(BF16)
    rest = table - high.astype(F32)
    middle = rest.astype(BF16)
    low = (rest - middle.astype(F32)).astype(BF16)
    pieces = jnp.concatenate([high, middle, low], axis=0)
    row_of = iota((chips * NC * NC, ROWS), 0)
    lane_of = iota((128, ROWS), 0).astype(F32)
    pair = []
    target = jnp.zeros((1, ROWS), F32)
    for k in range(TOP):
        route = routes[k : k + 1, :]
        slot = jnp.sum(jnp.where(route == block, slots, 0.0), axis=0, keepdims=True)
        line = ((route >> 4) * NC + core) * NC + other(core, (route >> 3) & 1)
        hot = jnp.where(line == row_of, 1.0, 0.0).astype(BF16)
        found = lax.dot_general(
            pieces,
            jnp.concatenate([hot, hot, hot], axis=0),
            (((0,), (0,)), ((), ())),
            preferred_element_type=F32,
        )
        pair.append(jnp.sum(jnp.where(lane_of == slot, found, 0.0), axis=0, keepdims=True))
        target = target + jnp.sum(
            jnp.where(lane_of == slot + 64.0, found, 0.0), axis=0, keepdims=True
        )
    pair = jnp.concatenate(pair, axis=0)
    top = jnp.max(pair, axis=0, keepdims=True)
    fine_lse = top + jnp.log(jnp.sum(jnp.exp(pair - top), axis=0, keepdims=True))
    log_prob = pair - fine_lse
    prob = jnp.exp(log_prob)

    parts = coarse_ref[0]
    tops = [parts[2 * i : 2 * i + 1] for i in range(NZ)]
    peak = tops[0]
    for line in tops[1:]:
        peak = jnp.maximum(peak, line)
    total = jnp.zeros((1, ROWS), F32)
    for i in range(NZ):
        total = total + parts[2 * i + 1 : 2 * i + 2] * jnp.exp(tops[i] - peak)
    picked = parts[16:24] - (peak + jnp.log(total))
    kl = jnp.sum(prob * (log_prob - picked), axis=0, keepdims=True)
    loss_ref[...] = fine_lse - target + kl
    prob_ref[...] = prob


def params(**more):
    return pltpu.CompilerParams(vmem_limit_bytes=VMEM, **more)


def smem():
    return pl.BlockSpec(memory_space=pltpu.SMEM)


def shape(dims, kind):
    return jax.ShapeDtypeStruct(dims, kind)


def swap(value, axes, split=0):
    return lax.all_to_all(value, axes, split, split, tiled=True)


def local(features, coarse_weight, fine_weight, block_cluster, routes, target_route, target_offset):
    ax = lax.axis_index
    at = jnp.stack([ax("x"), ax("z"), ax("c"), ax("hid")]).astype(I32)
    hbm = pl.BlockSpec(memory_space=pl.ANY)
    routes_t = routes.T

    full = lambda *dims: pl.BlockSpec(dims, lambda i: (0,) * len(dims))

    def run(kernel, specs, out, *operands, out_specs=None, scratch=(), **more):
        outs = out if isinstance(out, list) else [out]
        specs = [full(*o.shape) if spec is None else spec for spec, o in zip(specs, operands)]
        return pl.pallas_call(
            kernel,
            grid=(1,),
            in_specs=specs,
            out_specs=out_specs or [full(*o.shape) for o in outs],
            out_shape=outs,
            scratch_shapes=scratch,
            compiler_params=params(),
            **more,
        )(*operands)

    (here,) = run(
        pack_kernel,
        [None] * 5,
        shape((EXT, PART), BF16),
        features,
        routes_t,
        target_route[None],
        target_offset[None],
        block_cluster[None],
    )
    up = [(i, (i + 1) % NZ) for i in range(NZ)]
    down = [(i, (i - 1) % NZ) for i in range(NZ)]
    from_up, from_down = [here], [here]
    for step in range(NZ // 2):
        if step < NZ // 2 - 1:
            from_up.append(lax.ppermute(from_up[-1], "z", down))
        from_down.append(lax.ppermute(from_down[-1], "z", up))
    peer_weight = lax.ppermute(fine_weight, "c", [(0, 1), (1, 0)])
    coarse_t = lax.all_gather(coarse_weight.T, ("x", "c"), axis=0, tiled=True)
    columns = coarse_t.shape[0]

    near = (here, from_up[1], from_down[1], from_up[2])
    far = (from_down[2], from_up[3], from_down[3], from_down[4])
    tiers = NC * TIERS + 1
    last_run = [here]

    def in_turn(call, first, *more):
        first, _ = lax.optimization_barrier((first, last_run[0]))
        (last_run[0],) = call(first, *more)
        return last_run[0]

    def select(four, *waits):
        out = shape((NX, tiers, FOUR, PART), BF16)
        block = (NX, tiers, PAIR, PART)

        def begin(a, b):
            to = pl.BlockSpec(block, lambda i: (0, 0, 0, 0))
            return run(select_kernel, [smem(), None, None], out, at, a, b, out_specs=[to])

        def end(a, b, begun):
            to = pl.BlockSpec(block, lambda i: (0, 0, 1, 0))
            specs = [smem(), None, None, hbm]
            return run(
                select_more_kernel,
                specs,
                out,
                at,
                a,
                b,
                begun,
                out_specs=[to],
                input_output_aliases={3: 0},
            )

        first = lax.optimization_barrier((four[0], waits[0]))[0]
        begun = in_turn(begin, first, four[1])
        first = lax.optimization_barrier((four[2], waits[1]))[0]
        return swap(in_turn(end, first, four[3], begun), "x")

    def partial(four, *waits):
        def call(*four):
            out = shape((columns, NX * ROWS), F32)
            return run(partial_kernel, [None] * 5, out, *four, coarse_t)

        first = lax.optimization_barrier((four[0], *waits))[0]
        out = in_turn(call, first, *four[1:])
        return lax.psum_scatter(out, "hid", scatter_dimension=0, tiled=True)

    info = pl.BlockSpec((INFO, WIDE), lambda i: (ROWS // INFO, 0))

    def coarse(kernel, part, four, out, *more):
        def call(c):
            specs = [smem(), None] + [info] * 4 + [None] * len(more)
            return run(kernel, specs, out, at, c, *four, *more)

        return in_turn(call, part)

    def fine(rows):
        def call(rows):
            return run(
                fine_kernel,
                [hbm, hbm, None],
                shape((NX, NC, TIERS, FOUR, LBL), F32),
                fine_weight,
                peer_weight,
                rows,
                scratch=[
                    pltpu.VMEM((QB, PART, LBL), BF16),
                    pltpu.VMEM((NX, TIERS, FOUR, LBL), F32),
                    pltpu.SemaphoreType.DMA((QB,)),
                ],
                cost_estimate=pl.CostEstimate(
                    flops=8 * 10**9, bytes_accessed=40 * 2**20, transcendentals=0
                ),
            )

        return in_turn(call, rows)

    meta = pl.BlockSpec((NX, 1, FOUR, PART), lambda i: (0, NC * TIERS, 0, 0))

    def scored(kernel, fine, rows, out, *before):
        def call(fine):
            specs = [smem(), None, meta] + [None] * len(before)
            return run(kernel, specs, out, at, fine, rows, *before)

        return in_turn(call, fine)

    rows_near = select(near, from_down[1], from_down[2])
    part_near = partial(near)
    rows_far = select(far, from_down[3], from_down[4])
    part_far = partial(far, rows_near)
    fine_near = lax.psum_scatter(fine(rows_near), "hid", scatter_dimension=0, tiled=True)
    lines = coarse(coarse_kernel, part_near, near, shape((NZ // 2, 16, ROWS), F32))
    lines = coarse(coarse_last_kernel, part_far, far, shape((NZ, 16, ROWS), F32), lines)
    shards = [
        lax.ppermute(lines, "hid", [(i, (i + d) % HID) for i in range(HID)]) for d in range(1, HID)
    ]

    def add_shards(*shards):
        return run(coarse_sum_kernel, [smem()] + [None] * 4, shape((NZ, 24, ROWS), F32), at, *shards)

    lines = in_turn(add_shards, lines, *shards)
    lines = lax.psum_scatter(lines, "z", scatter_dimension=0, tiled=True)
    fine_far = swap(fine(rows_far), "hid")
    first = scored(score_kernel, fine_near, rows_near, shape((8, LBL), F32))
    table = scored(
        score_last_kernel, fine_far, rows_far, shape((HID * NX * NZ * NC * NC, 128), F32), first
    )
    table = swap(table, ("hid", "x", "z", "c"))

    loss, prob = run(
        finish_kernel,
        [smem(), None, None, None],
        [shape((1, ROWS), F32), shape((TOP, ROWS), F32)],
        at,
        table,
        lines,
        routes_t,
    )
    return loss.reshape(ROWS), prob.T


def solution(mesh):
    fine_mesh = Mesh(mesh.devices.reshape(HID, NX, NZ, NC), ("hid", "x", "z", "c"))
    blk = ("x", "z", "c")
    placed = (P(blk, "hid"), P("hid", blk), P(blk, "hid", None), P(), P(blk, None), P(blk), P(blk))
    return jax.shard_map(
        local, mesh=fine_mesh, in_specs=placed, out_specs=(P(blk), P(blk, None)), check_vma=False
    )
```

```python
import jax
import jax.numpy as jnp
from jax import lax
from jax.experimental import pallas as pl
from jax.experimental.pallas import tpu as pltpu
from jax.sharding import Mesh, PartitionSpec as P

F32 = jnp.float32
BF16 = jnp.bfloat16
I32 = jnp.int32

HID, NX, NZ, NC = 4, 4, 8, 2
ROWS = 256
PART = 1024
TOP = 8
BLK = 8
QB = NC * BLK
CAP = 8
LBL = 256
INFO = 16
SLOTS = 48
TIERS = SLOTS // CAP
PAIR = 2 * CAP
WIDE = 2 * ROWS
AWAY = ((0, 1, -1, 2), (-2, 3, -3, 4))
FOUR = 2 * PAIR
ARRIVE = {0: range(0, 2), 2: range(2, BLK), BLK: range(BLK, QB)}
GROUPS = NC * NX
EXT = ROWS + INFO
VMEM = 56 * 1024 * 1024


def iota(shape, dim):
    return lax.broadcasted_iota(I32, shape, dim)


def dot(a, b):
    return jnp.dot(a, b, preferred_element_type=F32)


def strict_upper():
    return jnp.where(iota((ROWS, ROWS), 0) < iota((ROWS, ROWS), 1), 1.0, 0.0).astype(BF16)


def other(core, half):
    return core + half - 2 * core * half


def pack_kernel(f_ref, routes_ref, place_ref, offset_ref, cluster_ref, out_ref):
    out_ref[0:ROWS, :] = f_ref[...]
    routes = routes_ref[...]
    clusters = cluster_ref[...]
    count = clusters.shape[1]
    table = jnp.concatenate([clusters >> 6, clusters & 63, jnp.zeros((14, count), I32)], axis=0)
    table = table.astype(F32).astype(BF16)
    groups, columns = [], []
    blocks = iota((count, ROWS), 0)
    for k in range(TOP):
        hot = jnp.where(blocks == routes[k : k + 1, :], 1.0, 0.0).astype(BF16)
        found = dot(table, hot)
        groups.append(found[0:1, :])
        columns.append(found[1:2, :])
    places = [place_ref[...].astype(F32), offset_ref[...].astype(F32), jnp.zeros((6, ROWS), F32)]
    left = jnp.concatenate([(routes - 256).astype(F32)] + columns, axis=0)
    right = jnp.concatenate(groups + places, axis=0)
    rest = jnp.zeros((INFO, PART - WIDE), F32)
    out_ref[ROWS:EXT, :] = jnp.concatenate([left, right, rest], axis=1).astype(BF16)


def select_more_kernel(at_ref, a_ref, b_ref, begun_ref, rows_ref):
    select_kernel(at_ref, a_ref, b_ref, rows_ref)


def select_kernel(at_ref, a_ref, b_ref, rows_ref):
    z, core = at_ref[1], at_ref[2]
    count = GROUPS * BLK
    index = iota((count, ROWS), 0)
    device = ((index >> 3) & 3) * (NZ * NC) + z * NC + other(core, index >> 5)
    blocks = device * BLK + (index & 7)
    upper = strict_upper()
    ones = jnp.ones((ROWS, ROWS), BF16)
    row, col = iota((count, count), 0), iota((count, count), 1)
    before = jnp.where(((row >> 3) == (col >> 3)) & (col < row), 1.0, 0.0).astype(BF16)
    slot_of = iota((SLOTS, ROWS), 0).astype(F32)
    eye = iota((SLOTS, 128), 0) == iota((SLOTS, 128), 1)

    def as_line(column):
        return jnp.sum(jnp.where(eye, column, 0.0), axis=0, keepdims=True)

    picked, owners, places = [], [], []
    for g_ref in (a_ref, b_ref):
        info = g_ref[ROWS:EXT, 0:WIDE].astype(F32)
        routes = info[0:TOP, 0:ROWS].astype(I32) + 256
        place = info[TOP : TOP + 1, ROWS:].astype(I32)
        offset = info[TOP + 1 : TOP + 2, ROWS:]
        hit = jnp.zeros((count, ROWS), F32)
        target = jnp.zeros((1, ROWS), I32)
        for k in range(TOP):
            hit = jnp.where(routes[k : k + 1, :] == blocks, 1.0, hit)
            target = jnp.where(place == k, routes[k : k + 1, :], target)
        held = hit.astype(BF16)
        start = dot(before, dot(held, ones).astype(BF16))
        slot = jnp.where(hit > 0.5, dot(held, upper) + start, -1.0)
        wanted = jnp.where(blocks == target, slot, -1.0)
        hots = []
        for g in range(GROUPS):
            label = jnp.full((SLOTS, ROWS), -1.0, F32)
            for b in range(BLK):
                label = jnp.where(slot[g * BLK + b : g * BLK + b + 1, :] == slot_of, float(b), label)
            hots.append(jnp.where(label > -0.5, 1.0, 0.0).astype(BF16))
            owners.append(as_line(jnp.max(label, axis=1, keepdims=True)))
            mine = jnp.max(wanted[g * BLK : (g + 1) * BLK, :], axis=0, keepdims=True)
            places.append(
                as_line(
                    jnp.sum(jnp.where(mine == slot_of, offset + 1.0, 0.0), axis=1, keepdims=True)
                )
            )
        hots = jnp.concatenate(hots, axis=0)
        picked.append(dot(hots, g_ref[0:ROWS, :]).reshape(GROUPS, TIERS, CAP, PART))
    both = jnp.concatenate(picked, axis=2).astype(BF16)
    for g in range(GROUPS):
        rows_ref[g % NX, (g // NX) * TIERS : (g // NX + 1) * TIERS] = both[g]
    for d in range(NX):
        lines = []
        for half in range(NC):
            g = half * NX + d
            lines += [owners[g], owners[GROUPS + g], places[g], places[GROUPS + g]]
        lines = jnp.concatenate(lines + [jnp.zeros((8, 128), F32)], axis=0)
        lines = jnp.concatenate([lines, jnp.zeros((PAIR, PART - 128), F32)], axis=1)
        rows_ref[d, NC * TIERS] = lines.astype(BF16)


def partial_kernel(a_ref, b_ref, c_ref, d_ref, w_ref, out_ref):
    for s, ref in enumerate((a_ref, b_ref, c_ref, d_ref)):
        out_ref[:, s * ROWS : (s + 1) * ROWS] = lax.dot_general(
            w_ref[...], ref[0:ROWS, :], (((1,), (1,)), ((), ())), preferred_element_type=F32
        )


def slot_lines(meta, half, kind):
    eye = iota((SLOTS, 128), 0) == iota((SLOTS, 128), 1)
    columns = []
    for s in range(4):
        at = (s // 2) * PAIR + half * 4 + kind * 2 + s % 2
        column = jnp.sum(jnp.where(eye, meta[at : at + 1, :], 0.0), axis=1, keepdims=True)
        columns.append(jnp.broadcast_to(column, (SLOTS, LBL)))
    return jnp.concatenate(
        [c[t * CAP : (t + 1) * CAP, :] for t in range(TIERS) for c in columns], axis=0
    )


def fine_kernel(own_ref, peer_ref, r_ref, out_ref, held_ref, owner_ref, sems):
    copies = []
    for i in range(QB):
        source = own_ref if i < BLK else peer_ref
        copies.append(pltpu.make_async_copy(source.at[i % BLK], held_ref.at[i], sems.at[i]))
        copies[i].start()
    for half in range(NC):
        for x in range(NX):
            meta = r_ref[x, NC * TIERS, :, 0:128].astype(F32)
            owner_ref[x] = slot_lines(meta, half, 0).reshape(TIERS, FOUR, LBL)
        for b in range(BLK):
            for i in ARRIVE.get(half * BLK + b, ()):
                copies[i].wait()
            end = min(b + 1, TIERS)
            rows = r_ref[:, half * TIERS : half * TIERS + end].reshape(NX * end * FOUR, PART)
            part = dot(rows, held_ref[half * BLK + b])
            for x in range(NX):
                for t in range(end):
                    at = (x * end + t) * FOUR
                    piece = part[at : at + FOUR]
                    if t < b:
                        piece = jnp.where(owner_ref[x, t] == float(b), piece, out_ref[x, half, t])
                    out_ref[x, half, t] = piece


def score(y, h, meta_ref):
    rows = NC * TIERS * FOUR
    y = y.reshape(rows, LBL)
    meta = meta_ref[h, 0, :, 0:128].astype(F32)
    wanted = jnp.concatenate([slot_lines(meta, half, 1) for half in range(NC)], axis=0)
    label = iota((rows, LBL), 1).astype(F32) + 1.0
    top = jnp.max(y, axis=1, keepdims=True)
    mass = top + jnp.log(jnp.sum(jnp.exp(y - top), axis=1, keepdims=True))
    target = jnp.sum(jnp.where(label == wanted, y, 0.0), axis=1, keepdims=True)
    order = iota((rows, LBL), 0)
    tier = order // FOUR
    half = jnp.where(tier >= TIERS, 1, 0)
    slot = half * 128 + (tier - half * TIERS) * CAP + (order & 7)
    lane = iota((rows, LBL), 1)
    packed = jnp.where(lane == slot, mass, 0.0) + jnp.where(lane == slot + 64, target, 0.0)
    packed = jnp.sum(packed.reshape(NC * TIERS, 4, CAP, LBL), axis=2)
    return jnp.sum(packed, axis=0)


def score_kernel(at_ref, y_ref, meta_ref, out_ref):
    out_ref[0:4, :] = score(y_ref[0], at_ref[3], meta_ref)
    out_ref[4:8, :] = jnp.zeros((4, LBL), F32)


def score_last_kernel(at_ref, y_ref, meta_ref, first_ref, out_ref):
    z, core, h = at_ref[1], at_ref[2], at_ref[3]
    y = y_ref[0] + y_ref[1] + y_ref[2] + y_ref[3]
    last = score(y, h, meta_ref)
    out_ref[...] = jnp.zeros_like(out_ref)
    for i, lines in enumerate((first_ref, last)):
        for s in range(4):
            to = (z + NZ + AWAY[i][s]) & (NZ - 1)
            for d in range(HID):
                at = (((d * NX + h) * NZ + to) * NC + core) * NC
                for half in range(NC):
                    line = lines[s : s + 1, half * 128 : (half + 1) * 128]
                    out_ref[pl.ds(at + half, 1), :] = line


def coarse_lines(at_ref, c_ref, infos):
    z, h = at_ref[1], at_ref[3]
    width = c_ref.shape[0]
    column = iota((width, ROWS), 0)
    out = []
    for s, info_ref in enumerate(infos):
        logits = c_ref[:, s * ROWS : (s + 1) * ROWS]
        info = info_ref[...].astype(F32).astype(I32)
        inside = info[TOP : 2 * TOP, 0:ROWS]
        group = info[0:TOP, ROWS:WIDE]
        place = ((group >> 4) * NC + (group & 1)) * 64 + inside - h * width
        place = jnp.where(((group >> 1) & 7) == z, place, -1)
        top = jnp.max(logits, axis=0, keepdims=True)
        total = jnp.sum(jnp.exp(logits - top), axis=0, keepdims=True)
        lines = [top, total, jnp.zeros((6, ROWS), F32)]
        for k in range(TOP):
            lines.append(
                jnp.sum(
                    jnp.where(column == place[k : k + 1, :], logits, 0.0), axis=0, keepdims=True
                )
            )
        out.append(jnp.concatenate(lines, axis=0))
    return out


def coarse_kernel(at_ref, c_ref, i0, i1, i2, i3, out_ref):
    for s, lines in enumerate(coarse_lines(at_ref, c_ref, (i0, i1, i2, i3))):
        out_ref[s] = lines


def coarse_last_kernel(at_ref, c_ref, i0, i1, i2, i3, first_ref, out_ref):
    last = coarse_lines(at_ref, c_ref, (i0, i1, i2, i3))
    for i in range(NZ):
        out_ref[i] = first_ref[i] if i < NZ // 2 else last[i - NZ // 2]


def coarse_sum_kernel(own_ref, next_ref, across_ref, before_ref, *out_refs):
    for i, out_ref in enumerate(out_refs):
        shards = [ref[i] for ref in (own_ref, across_ref, next_ref, before_ref)]
        top = shards[0][0:1]
        for shard in shards[1:]:
            top = jnp.maximum(top, shard[0:1])
        sums = [shard[1:2] * jnp.exp(shard[0:1] - top) for shard in shards]
        picks = [shard[8:16] for shard in shards]
        out_ref[0:8, :] = jnp.concatenate(
            [top, (sums[0] + sums[1]) + (sums[2] + sums[3]), jnp.zeros((6, ROWS), F32)], axis=0
        )
        out_ref[8:16, :] = (picks[0] + picks[1]) + (picks[2] + picks[3])


def finish_kernel(at_ref, fine_ref, *refs):
    *coarse_refs, routes_ref, loss_ref, prob_ref = refs
    x, core = at_ref[0], at_ref[2]
    routes = routes_ref[...]
    chips = NX * NZ
    index = iota((QB * chips, ROWS), 0)
    q = index >> 5
    block = ((index & 31) * NC + other(core, q >> 3)) * BLK + (q & 7)
    hit = jnp.zeros((QB * chips, ROWS), F32)
    for k in range(TOP):
        hit = jnp.where(routes[k : k + 1, :] == block, 1.0, hit)
    held = hit.astype(BF16)
    rank = dot(held, strict_upper())
    count = dot(held, jnp.ones((ROWS, ROWS), BF16))
    slots = []
    for half in range(NC):
        start = jnp.zeros((chips, ROWS), F32)
        for b in range(BLK):
            at = (half * BLK + b) * chips
            slots.append(rank[at : at + chips] + start)
            start = start + count[at : at + chips]
    slots = jnp.concatenate(slots, axis=0)

    table = fine_ref[pl.ds(x * (chips * NC * NC), chips * NC * NC), :]
    high = table.astype(BF16)
    rest = table - high.astype(F32)
    middle = rest.astype(BF16)
    low = (rest - middle.astype(F32)).astype(BF16)
    pieces = jnp.concatenate([high, middle, low], axis=0)
    row_of = iota((chips * NC * NC, ROWS), 0)
    lane_of = iota((128, ROWS), 0).astype(F32)
    pair = []
    target = jnp.zeros((1, ROWS), F32)
    for k in range(TOP):
        route = routes[k : k + 1, :]
        slot = jnp.sum(jnp.where(route == block, slots, 0.0), axis=0, keepdims=True)
        line = ((route >> 4) * NC + core) * NC + other(core, (route >> 3) & 1)
        hot = jnp.where(line == row_of, 1.0, 0.0).astype(BF16)
        found = lax.dot_general(
            pieces,
            jnp.concatenate([hot, hot, hot], axis=0),
            (((0,), (0,)), ((), ())),
            preferred_element_type=F32,
        )
        pair.append(jnp.sum(jnp.where(lane_of == slot, found, 0.0), axis=0, keepdims=True))
        target = target + jnp.sum(
            jnp.where(lane_of == slot + 64.0, found, 0.0), axis=0, keepdims=True
        )
    pair = jnp.concatenate(pair, axis=0)
    top = jnp.max(pair, axis=0, keepdims=True)
    fine_lse = top + jnp.log(jnp.sum(jnp.exp(pair - top), axis=0, keepdims=True))
    log_prob = pair - fine_lse
    prob = jnp.exp(log_prob)

    parts = [ref[...] for ref in coarse_refs]
    peak = parts[0][0:1]
    for part in parts[1:]:
        peak = jnp.maximum(peak, part[0:1])
    total = jnp.zeros((1, ROWS), F32)
    picked = jnp.zeros((TOP, ROWS), F32)
    for part in parts:
        total = total + part[1:2] * jnp.exp(part[0:1] - peak)
        picked = picked + part[8:16]
    picked = picked - (peak + jnp.log(total))
    kl = jnp.sum(prob * (log_prob - picked), axis=0, keepdims=True)
    loss_ref[...] = fine_lse - target + kl
    prob_ref[...] = prob


def params(**more):
    return pltpu.CompilerParams(vmem_limit_bytes=VMEM, **more)


def smem():
    return pl.BlockSpec(memory_space=pltpu.SMEM)


def shape(dims, kind):
    return jax.ShapeDtypeStruct(dims, kind)


def swap(value, axes, split=0):
    return lax.all_to_all(value, axes, split, split, tiled=True)


def local(features, coarse_weight, fine_weight, block_cluster, routes, target_route, target_offset):
    ax = lax.axis_index
    at = jnp.stack([ax("x"), ax("z"), ax("c"), ax("hid")]).astype(I32)
    hbm = pl.BlockSpec(memory_space=pl.ANY)
    routes_t = routes.T

    full = lambda *dims: pl.BlockSpec(dims, lambda i: (0,) * len(dims))

    def run(kernel, specs, out, *operands, out_specs=None, scratch=(), **more):
        outs = out if isinstance(out, list) else [out]
        specs = [full(*o.shape) if spec is None else spec for spec, o in zip(specs, operands)]
        return pl.pallas_call(
            kernel,
            grid=(1,),
            in_specs=specs,
            out_specs=out_specs or [full(*o.shape) for o in outs],
            out_shape=outs,
            scratch_shapes=scratch,
            compiler_params=params(),
            **more,
        )(*operands)

    (here,) = run(
        pack_kernel,
        [None] * 5,
        shape((EXT, PART), BF16),
        features,
        routes_t,
        target_route[None],
        target_offset[None],
        block_cluster[None],
    )
    up = [(i, (i + 1) % NZ) for i in range(NZ)]
    down = [(i, (i - 1) % NZ) for i in range(NZ)]
    from_up, from_down = [here], [here]
    for step in range(NZ // 2):
        if step < NZ // 2 - 1:
            from_up.append(lax.ppermute(from_up[-1], "z", down))
        from_down.append(lax.ppermute(from_down[-1], "z", up))
    peer_weight = lax.ppermute(fine_weight, "c", [(0, 1), (1, 0)])
    coarse_t = lax.all_gather(coarse_weight.T, ("x", "c"), axis=0, tiled=True)
    columns = coarse_t.shape[0]

    near = (here, from_up[1], from_down[1], from_up[2])
    far = (from_down[2], from_up[3], from_down[3], from_down[4])
    tiers = NC * TIERS + 1
    last_run = [here]

    def in_turn(call, first, *more):
        first, _ = lax.optimization_barrier((first, last_run[0]))
        (last_run[0],) = call(first, *more)
        return last_run[0]

    def select(four, *waits):
        out = shape((NX, tiers, FOUR, PART), BF16)
        block = (NX, tiers, PAIR, PART)

        def begin(a, b):
            to = pl.BlockSpec(block, lambda i: (0, 0, 0, 0))
            return run(select_kernel, [smem(), None, None], out, at, a, b, out_specs=[to])

        def end(a, b, begun):
            to = pl.BlockSpec(block, lambda i: (0, 0, 1, 0))
            specs = [smem(), None, None, hbm]
            return run(
                select_more_kernel,
                specs,
                out,
                at,
                a,
                b,
                begun,
                out_specs=[to],
                input_output_aliases={3: 0},
            )

        first = lax.optimization_barrier((four[0], waits[0]))[0]
        begun = in_turn(begin, first, four[1])
        first = lax.optimization_barrier((four[2], waits[1]))[0]
        return swap(in_turn(end, first, four[3], begun), "x")

    def partial(four, *waits):
        def call(*four):
            out = shape((columns, NX * ROWS), F32)
            return run(partial_kernel, [None] * 5, out, *four, coarse_t)

        first = lax.optimization_barrier((four[0], *waits))[0]
        out = in_turn(call, first, *four[1:])
        return lax.psum_scatter(out, "hid", scatter_dimension=0, tiled=True)

    info = pl.BlockSpec((INFO, WIDE), lambda i: (ROWS // INFO, 0))

    def coarse(kernel, part, four, out, *more):
        def call(c):
            specs = [smem(), None] + [info] * 4 + [None] * len(more)
            return run(kernel, specs, out, at, c, *four, *more)

        return in_turn(call, part)

    def fine(rows):
        def call(rows):
            return run(
                fine_kernel,
                [hbm, hbm, None],
                shape((NX, NC, TIERS, FOUR, LBL), F32),
                fine_weight,
                peer_weight,
                rows,
                scratch=[
                    pltpu.VMEM((QB, PART, LBL), BF16),
                    pltpu.VMEM((NX, TIERS, FOUR, LBL), F32),
                    pltpu.SemaphoreType.DMA((QB,)),
                ],
                cost_estimate=pl.CostEstimate(
                    flops=8 * 10**9, bytes_accessed=40 * 2**20, transcendentals=0
                ),
            )

        return in_turn(call, rows)

    meta = pl.BlockSpec((NX, 1, FOUR, PART), lambda i: (0, NC * TIERS, 0, 0))

    def scored(kernel, fine, rows, out, *before):
        def call(fine):
            specs = [smem(), None, meta] + [None] * len(before)
            return run(kernel, specs, out, at, fine, rows, *before)

        return in_turn(call, fine)

    rows_near = select(near, from_down[1], from_down[2])
    part_near = partial(near)
    rows_far = select(far, from_down[3], from_down[4])
    part_far = partial(far, rows_near)
    fine_near = lax.psum_scatter(fine(rows_near), "hid", scatter_dimension=0, tiled=True)
    lines = coarse(coarse_kernel, part_near, near, shape((NZ // 2, 16, ROWS), F32))
    lines = coarse(coarse_last_kernel, part_far, far, shape((NZ, 16, ROWS), F32), lines)
    shards = [
        lax.ppermute(lines, "hid", [(i, (i + d) % HID) for i in range(HID)]) for d in range(1, HID)
    ]

    fine_far = fine(rows_far)
    first, _ = lax.optimization_barrier((lines, fine_far))
    lines = run(
        coarse_sum_kernel, [None] * 4, [shape((16, ROWS), F32)] * NZ, first, *shards
    )
    last_run[0] = lines[0]
    away = [d for four in AWAY for d in four]
    lines = [
        lax.ppermute(part, "z", [(i, (i + d) % NZ) for i in range(NZ)]) if d else part
        for part, d in zip(lines, away)
    ]
    fine_far = swap(fine_far, "hid")
    first = scored(score_kernel, fine_near, rows_near, shape((8, LBL), F32))
    fine_far, *lines = lax.optimization_barrier((fine_far, *lines))
    table = scored(
        score_last_kernel, fine_far, rows_far, shape((HID * NX * NZ * NC * NC, 128), F32), first
    )
    table = swap(table, ("hid", "x", "z", "c"))

    loss, prob = run(
        finish_kernel,
        [smem()] + [None] * (NZ + 2),
        [shape((1, ROWS), F32), shape((TOP, ROWS), F32)],
        at,
        table,
        *lines,
        routes_t,
    )
    return loss.reshape(ROWS), prob.T


def solution(mesh):
    fine_mesh = Mesh(mesh.devices.reshape(HID, NX, NZ, NC), ("hid", "x", "z", "c"))
    blk = ("x", "z", "c")
    placed = (P(blk, "hid"), P("hid", blk), P(blk, "hid", None), P(), P(blk, None), P(blk), P(blk))
    return jax.shard_map(
        local, mesh=fine_mesh, in_specs=placed, out_specs=(P(blk), P(blk, None)), check_vma=False
    )
```

```python
import jax
import jax.numpy as jnp
from jax import lax
from jax.experimental import pallas as pl
from jax.experimental.pallas import tpu as pltpu
from jax.sharding import Mesh, PartitionSpec as P

F32 = jnp.float32
BF16 = jnp.bfloat16
I32 = jnp.int32

HID, NX, NZ, NC = 4, 4, 8, 2
ROWS = 256
PART = 1024
TOP = 8
BLK = 8
QB = NC * BLK
CAP = 8
LBL = 256
INFO = 16
SLOTS = 48
TIERS = SLOTS // CAP
PAIR = 2 * CAP
WIDE = 2 * ROWS
AWAY = ((0, 1, -1, 2), (-2, 3, -3, 4))
FOUR = 2 * PAIR
ARRIVE = {0: range(0, 2), 2: range(2, BLK), BLK: range(BLK, QB)}
GROUPS = NC * NX
EXT = ROWS + INFO
VMEM = 56 * 1024 * 1024


def iota(shape, dim):
    return lax.broadcasted_iota(I32, shape, dim)


def dot(a, b):
    return jnp.dot(a, b, preferred_element_type=F32)


def strict_upper():
    return jnp.where(iota((ROWS, ROWS), 0) < iota((ROWS, ROWS), 1), 1.0, 0.0).astype(BF16)


def other(core, half):
    return core + half - 2 * core * half


def pack_kernel(f_ref, routes_ref, place_ref, offset_ref, cluster_ref, out_ref):
    out_ref[0:ROWS, :] = f_ref[...]
    routes = routes_ref[...]
    clusters = cluster_ref[...]
    count = clusters.shape[1]
    table = jnp.concatenate([clusters >> 6, clusters & 63, jnp.zeros((14, count), I32)], axis=0)
    table = table.astype(F32).astype(BF16)
    groups, columns = [], []
    blocks = iota((count, ROWS), 0)
    for k in range(TOP):
        hot = jnp.where(blocks == routes[k : k + 1, :], 1.0, 0.0).astype(BF16)
        found = dot(table, hot)
        groups.append(found[0:1, :])
        columns.append(found[1:2, :])
    places = [place_ref[...].astype(F32), offset_ref[...].astype(F32), jnp.zeros((6, ROWS), F32)]
    left = jnp.concatenate([(routes - 256).astype(F32)] + columns, axis=0)
    right = jnp.concatenate(groups + places, axis=0)
    rest = jnp.zeros((INFO, PART - WIDE), F32)
    out_ref[ROWS:EXT, :] = jnp.concatenate([left, right, rest], axis=1).astype(BF16)


def select_more_kernel(at_ref, a_ref, b_ref, begun_ref, rows_ref):
    select_kernel(at_ref, a_ref, b_ref, rows_ref)


def select_kernel(at_ref, a_ref, b_ref, rows_ref):
    z, core = at_ref[1], at_ref[2]
    count = GROUPS * BLK
    index = iota((count, ROWS), 0)
    device = ((index >> 3) & 3) * (NZ * NC) + z * NC + other(core, index >> 5)
    blocks = device * BLK + (index & 7)
    upper = strict_upper()
    ones = jnp.ones((ROWS, ROWS), BF16)
    row, col = iota((count, count), 0), iota((count, count), 1)
    before = jnp.where(((row >> 3) == (col >> 3)) & (col < row), 1.0, 0.0).astype(BF16)
    slot_of = iota((SLOTS, ROWS), 0).astype(F32)
    eye = iota((SLOTS, 128), 0) == iota((SLOTS, 128), 1)

    def as_line(column):
        return jnp.sum(jnp.where(eye, column, 0.0), axis=0, keepdims=True)

    picked, owners, places = [], [], []
    for g_ref in (a_ref, b_ref):
        info = g_ref[ROWS:EXT, 0:WIDE].astype(F32)
        routes = info[0:TOP, 0:ROWS].astype(I32) + 256
        place = info[TOP : TOP + 1, ROWS:].astype(I32)
        offset = info[TOP + 1 : TOP + 2, ROWS:]
        hit = jnp.zeros((count, ROWS), F32)
        target = jnp.zeros((1, ROWS), I32)
        for k in range(TOP):
            hit = jnp.where(routes[k : k + 1, :] == blocks, 1.0, hit)
            target = jnp.where(place == k, routes[k : k + 1, :], target)
        held = hit.astype(BF16)
        start = dot(before, dot(held, ones).astype(BF16))
        slot = jnp.where(hit > 0.5, dot(held, upper) + start, -1.0)
        wanted = jnp.where(blocks == target, slot, -1.0)
        hots = []
        for g in range(GROUPS):
            label = jnp.full((SLOTS, ROWS), -1.0, F32)
            for b in range(BLK):
                label = jnp.where(slot[g * BLK + b : g * BLK + b + 1, :] == slot_of, float(b), label)
            hots.append(jnp.where(label > -0.5, 1.0, 0.0).astype(BF16))
            owners.append(as_line(jnp.max(label, axis=1, keepdims=True)))
            mine = jnp.max(wanted[g * BLK : (g + 1) * BLK, :], axis=0, keepdims=True)
            places.append(
                as_line(
                    jnp.sum(jnp.where(mine == slot_of, offset + 1.0, 0.0), axis=1, keepdims=True)
                )
            )
        hots = jnp.concatenate(hots, axis=0)
        picked.append(dot(hots, g_ref[0:ROWS, :]).reshape(GROUPS, TIERS, CAP, PART))
    both = jnp.concatenate(picked, axis=2).astype(BF16)
    for g in range(GROUPS):
        rows_ref[g % NX, (g // NX) * TIERS : (g // NX + 1) * TIERS] = both[g]
    for d in range(NX):
        lines = []
        for half in range(NC):
            g = half * NX + d
            lines += [owners[g], owners[GROUPS + g], places[g], places[GROUPS + g]]
        lines = jnp.concatenate(lines + [jnp.zeros((8, 128), F32)], axis=0)
        lines = jnp.concatenate([lines, jnp.zeros((PAIR, PART - 128), F32)], axis=1)
        rows_ref[d, NC * TIERS] = lines.astype(BF16)


def partial_kernel(a_ref, b_ref, c_ref, d_ref, w_ref, out_ref):
    for s, ref in enumerate((a_ref, b_ref, c_ref, d_ref)):
        out_ref[:, s * ROWS : (s + 1) * ROWS] = lax.dot_general(
            w_ref[...], ref[0:ROWS, :], (((1,), (1,)), ((), ())), preferred_element_type=F32
        )


def slot_lines(meta, half, kind):
    eye = iota((SLOTS, 128), 0) == iota((SLOTS, 128), 1)
    columns = []
    for s in range(4):
        at = (s // 2) * PAIR + half * 4 + kind * 2 + s % 2
        column = jnp.sum(jnp.where(eye, meta[at : at + 1, :], 0.0), axis=1, keepdims=True)
        columns.append(jnp.broadcast_to(column, (SLOTS, LBL)))
    return jnp.concatenate(
        [c[t * CAP : (t + 1) * CAP, :] for t in range(TIERS) for c in columns], axis=0
    )


def fine_kernel(own_ref, peer_ref, r_ref, out_ref, held_ref, owner_ref, sems):
    copies = []
    for i in range(QB):
        source = own_ref if i < BLK else peer_ref
        copies.append(pltpu.make_async_copy(source.at[i % BLK], held_ref.at[i], sems.at[i]))
        copies[i].start()
    for half in range(NC):
        for x in range(NX):
            meta = r_ref[x, NC * TIERS, :, 0:128].astype(F32)
            owner_ref[x] = slot_lines(meta, half, 0).reshape(TIERS, FOUR, LBL)
        for b in range(BLK):
            for i in ARRIVE.get(half * BLK + b, ()):
                copies[i].wait()
            end = min(b + 1, TIERS)
            rows = r_ref[:, half * TIERS : half * TIERS + end].reshape(NX * end * FOUR, PART)
            part = dot(rows, held_ref[half * BLK + b])
            for x in range(NX):
                for t in range(end):
                    at = (x * end + t) * FOUR
                    piece = part[at : at + FOUR]
                    if t < b:
                        piece = jnp.where(owner_ref[x, t] == float(b), piece, out_ref[x, half, t])
                    out_ref[x, half, t] = piece


def score(y, h, meta_ref):
    rows = NC * TIERS * FOUR
    y = y.reshape(rows, LBL)
    meta = meta_ref[h, 0, :, 0:128].astype(F32)
    wanted = jnp.concatenate([slot_lines(meta, half, 1) for half in range(NC)], axis=0)
    label = iota((rows, LBL), 1).astype(F32) + 1.0
    top = jnp.max(y, axis=1, keepdims=True)
    mass = top + jnp.log(jnp.sum(jnp.exp(y - top), axis=1, keepdims=True))
    target = jnp.sum(jnp.where(label == wanted, y, 0.0), axis=1, keepdims=True)
    order = iota((rows, LBL), 0)
    tier = order // FOUR
    half = jnp.where(tier >= TIERS, 1, 0)
    slot = half * 128 + (tier - half * TIERS) * CAP + (order & 7)
    lane = iota((rows, LBL), 1)
    packed = jnp.where(lane == slot, mass, 0.0) + jnp.where(lane == slot + 64, target, 0.0)
    packed = jnp.sum(packed.reshape(NC * TIERS, 4, CAP, LBL), axis=2)
    return jnp.sum(packed, axis=0)


def score_kernel(at_ref, y_ref, meta_ref, out_ref):
    out_ref[0:4, :] = score(y_ref[0], at_ref[3], meta_ref)
    out_ref[4:8, :] = jnp.zeros((4, LBL), F32)


def score_last_kernel(at_ref, y_ref, meta_ref, first_ref, out_ref):
    z, core, h = at_ref[1], at_ref[2], at_ref[3]
    y = y_ref[0] + y_ref[1] + y_ref[2] + y_ref[3]
    last = score(y, h, meta_ref)
    out_ref[...] = jnp.zeros_like(out_ref)
    for i, lines in enumerate((first_ref, last)):
        for s in range(4):
            to = (z + NZ + AWAY[i][s]) & (NZ - 1)
            for d in range(HID):
                at = (((d * NX + h) * NZ + to) * NC + core) * NC
                for half in range(NC):
                    line = lines[s : s + 1, half * 128 : (half + 1) * 128]
                    out_ref[pl.ds(at + half, 1), :] = line


def coarse_lines(at_ref, c_ref, infos):
    z, h = at_ref[1], at_ref[3]
    width = c_ref.shape[0]
    column = iota((width, ROWS), 0)
    out = []
    for s, info_ref in enumerate(infos):
        logits = c_ref[:, s * ROWS : (s + 1) * ROWS]
        info = info_ref[...].astype(F32).astype(I32)
        inside = info[TOP : 2 * TOP, 0:ROWS]
        group = info[0:TOP, ROWS:WIDE]
        place = ((group >> 4) * NC + (group & 1)) * 64 + inside - h * width
        place = jnp.where(((group >> 1) & 7) == z, place, -1)
        top = jnp.max(logits, axis=0, keepdims=True)
        total = jnp.sum(jnp.exp(logits - top), axis=0, keepdims=True)
        lines = [top, total, jnp.zeros((6, ROWS), F32)]
        for k in range(TOP):
            lines.append(
                jnp.sum(
                    jnp.where(column == place[k : k + 1, :], logits, 0.0), axis=0, keepdims=True
                )
            )
        out.append(jnp.concatenate(lines, axis=0))
    return out


def coarse_kernel(at_ref, c_ref, i0, i1, i2, i3, out_ref):
    for s, lines in enumerate(coarse_lines(at_ref, c_ref, (i0, i1, i2, i3))):
        out_ref[s] = lines


def coarse_last_kernel(at_ref, c_ref, i0, i1, i2, i3, first_ref, *out_refs):
    last = coarse_lines(at_ref, c_ref, (i0, i1, i2, i3))
    for i, out_ref in enumerate(out_refs):
        out_ref[...] = first_ref[i] if i < NZ // 2 else last[i - NZ // 2]


def joined(shards):
    top = shards[0][0:1]
    for shard in shards[1:]:
        top = jnp.maximum(top, shard[0:1])
    sums = [shard[1:2] * jnp.exp(shard[0:1] - top) for shard in shards]
    picks = [shard[8:16] for shard in shards]
    while len(sums) > 1:
        sums = [a + b for a, b in zip(sums[0::2], sums[1::2])]
        picks = [a + b for a, b in zip(picks[0::2], picks[1::2])]
    return top, sums[0], picks[0]


def coarse_sum_kernel(*refs):
    *shard_refs, out_ref = refs
    top, total, picked = joined([ref[...] for ref in shard_refs])
    out_ref[0:8, :] = jnp.concatenate([top, total, jnp.zeros((6, ROWS), F32)], axis=0)
    out_ref[8:16, :] = picked


def finish_kernel(at_ref, fine_ref, *refs):
    *coarse_refs, routes_ref, loss_ref, prob_ref = refs
    x, core = at_ref[0], at_ref[2]
    routes = routes_ref[...]
    chips = NX * NZ
    index = iota((QB * chips, ROWS), 0)
    q = index >> 5
    block = ((index & 31) * NC + other(core, q >> 3)) * BLK + (q & 7)
    hit = jnp.zeros((QB * chips, ROWS), F32)
    for k in range(TOP):
        hit = jnp.where(routes[k : k + 1, :] == block, 1.0, hit)
    held = hit.astype(BF16)
    rank = dot(held, strict_upper())
    count = dot(held, jnp.ones((ROWS, ROWS), BF16))
    slots = []
    for half in range(NC):
        start = jnp.zeros((chips, ROWS), F32)
        for b in range(BLK):
            at = (half * BLK + b) * chips
            slots.append(rank[at : at + chips] + start)
            start = start + count[at : at + chips]
    slots = jnp.concatenate(slots, axis=0)

    table = fine_ref[pl.ds(x * (chips * NC * NC), chips * NC * NC), :]
    high = table.astype(BF16)
    rest = table - high.astype(F32)
    middle = rest.astype(BF16)
    low = (rest - middle.astype(F32)).astype(BF16)
    pieces = jnp.concatenate([high, middle, low], axis=0)
    row_of = iota((chips * NC * NC, ROWS), 0)
    lane_of = iota((128, ROWS), 0).astype(F32)
    pair = []
    target = jnp.zeros((1, ROWS), F32)
    for k in range(TOP):
        route = routes[k : k + 1, :]
        slot = jnp.sum(jnp.where(route == block, slots, 0.0), axis=0, keepdims=True)
        line = ((route >> 4) * NC + core) * NC + other(core, (route >> 3) & 1)
        hot = jnp.where(line == row_of, 1.0, 0.0).astype(BF16)
        found = lax.dot_general(
            pieces,
            jnp.concatenate([hot, hot, hot], axis=0),
            (((0,), (0,)), ((), ())),
            preferred_element_type=F32,
        )
        pair.append(jnp.sum(jnp.where(lane_of == slot, found, 0.0), axis=0, keepdims=True))
        target = target + jnp.sum(
            jnp.where(lane_of == slot + 64.0, found, 0.0), axis=0, keepdims=True
        )
    pair = jnp.concatenate(pair, axis=0)
    top = jnp.max(pair, axis=0, keepdims=True)
    fine_lse = top + jnp.log(jnp.sum(jnp.exp(pair - top), axis=0, keepdims=True))
    log_prob = pair - fine_lse
    prob = jnp.exp(log_prob)

    top, total, picked = joined([ref[...] for ref in coarse_refs])
    picked = picked - (top + jnp.log(total))
    kl = jnp.sum(prob * (log_prob - picked), axis=0, keepdims=True)
    loss_ref[...] = fine_lse - target + kl
    prob_ref[...] = prob


def params(**more):
    return pltpu.CompilerParams(vmem_limit_bytes=VMEM, **more)


def smem():
    return pl.BlockSpec(memory_space=pltpu.SMEM)


def shape(dims, kind):
    return jax.ShapeDtypeStruct(dims, kind)


def swap(value, axes, split=0):
    return lax.all_to_all(value, axes, split, split, tiled=True)


def local(features, coarse_weight, fine_weight, block_cluster, routes, target_route, target_offset):
    ax = lax.axis_index
    at = jnp.stack([ax("x"), ax("z"), ax("c"), ax("hid")]).astype(I32)
    hbm = pl.BlockSpec(memory_space=pl.ANY)
    routes_t = routes.T

    full = lambda *dims: pl.BlockSpec(dims, lambda i: (0,) * len(dims))

    def run(kernel, specs, out, *operands, out_specs=None, scratch=(), **more):
        outs = out if isinstance(out, list) else [out]
        specs = [full(*o.shape) if spec is None else spec for spec, o in zip(specs, operands)]
        return pl.pallas_call(
            kernel,
            grid=(1,),
            in_specs=specs,
            out_specs=out_specs or [full(*o.shape) for o in outs],
            out_shape=outs,
            scratch_shapes=scratch,
            compiler_params=params(),
            **more,
        )(*operands)

    (here,) = run(
        pack_kernel,
        [None] * 5,
        shape((EXT, PART), BF16),
        features,
        routes_t,
        target_route[None],
        target_offset[None],
        block_cluster[None],
    )
    up = [(i, (i + 1) % NZ) for i in range(NZ)]
    down = [(i, (i - 1) % NZ) for i in range(NZ)]
    from_up, from_down = [here], [here]
    for step in range(NZ // 2):
        if step < NZ // 2 - 1:
            from_up.append(lax.ppermute(from_up[-1], "z", down))
        from_down.append(lax.ppermute(from_down[-1], "z", up))
    peer_weight = lax.ppermute(fine_weight, "c", [(0, 1), (1, 0)])
    coarse_t = lax.all_gather(coarse_weight.T, ("x", "c"), axis=0, tiled=True)
    columns = coarse_t.shape[0]

    near = (here, from_up[1], from_down[1], from_up[2])
    far = (from_down[2], from_up[3], from_down[3], from_down[4])
    tiers = NC * TIERS + 1
    last_run = [here]

    def in_turn(call, first, *more):
        first, _ = lax.optimization_barrier((first, last_run[0]))
        outs = call(first, *more)
        last_run[0] = outs[0]
        return outs if len(outs) > 1 else outs[0]

    def select(four, *waits):
        out = shape((NX, tiers, FOUR, PART), BF16)
        block = (NX, tiers, PAIR, PART)

        def begin(a, b):
            to = pl.BlockSpec(block, lambda i: (0, 0, 0, 0))
            return run(select_kernel, [smem(), None, None], out, at, a, b, out_specs=[to])

        def end(a, b, begun):
            to = pl.BlockSpec(block, lambda i: (0, 0, 1, 0))
            specs = [smem(), None, None, hbm]
            return run(
                select_more_kernel,
                specs,
                out,
                at,
                a,
                b,
                begun,
                out_specs=[to],
                input_output_aliases={3: 0},
            )

        first = lax.optimization_barrier((four[0], waits[0]))[0]
        begun = in_turn(begin, first, four[1])
        first = lax.optimization_barrier((four[2], waits[1]))[0]
        return swap(in_turn(end, first, four[3], begun), "x")

    def partial(four, *waits):
        def call(*four):
            out = shape((columns, NX * ROWS), F32)
            return run(partial_kernel, [None] * 5, out, *four, coarse_t)

        first = lax.optimization_barrier((four[0], *waits))[0]
        out = in_turn(call, first, *four[1:])
        return lax.psum_scatter(out, "hid", scatter_dimension=0, tiled=True)

    info = pl.BlockSpec((INFO, WIDE), lambda i: (ROWS // INFO, 0))

    def coarse(kernel, part, four, out, *more):
        def call(c):
            specs = [smem(), None] + [info] * 4 + [None] * len(more)
            return run(kernel, specs, out, at, c, *four, *more)

        return in_turn(call, part)

    def fine(rows):
        def call(rows):
            return run(
                fine_kernel,
                [hbm, hbm, None],
                shape((NX, NC, TIERS, FOUR, LBL), F32),
                fine_weight,
                peer_weight,
                rows,
                scratch=[
                    pltpu.VMEM((QB, PART, LBL), BF16),
                    pltpu.VMEM((NX, TIERS, FOUR, LBL), F32),
                    pltpu.SemaphoreType.DMA((QB,)),
                ],
                cost_estimate=pl.CostEstimate(
                    flops=8 * 10**9, bytes_accessed=40 * 2**20, transcendentals=0
                ),
            )

        return in_turn(call, rows)

    meta = pl.BlockSpec((NX, 1, FOUR, PART), lambda i: (0, NC * TIERS, 0, 0))

    def scored(kernel, fine, rows, out, *before):
        def call(fine):
            specs = [smem(), None, meta] + [None] * len(before)
            return run(kernel, specs, out, at, fine, rows, *before)

        return in_turn(call, fine)

    rows_near = select(near, from_down[1], from_down[2])
    part_near = partial(near)
    rows_far = select(far, from_down[3], from_down[4])
    part_far = partial(far, rows_near)
    fine_near = lax.psum_scatter(fine(rows_near), "hid", scatter_dimension=0, tiled=True)
    lines = coarse(coarse_kernel, part_near, near, shape((NZ // 2, 16, ROWS), F32))
    lines = coarse(
        coarse_last_kernel, part_far, far, [shape((16, ROWS), F32)] * NZ, lines
    )
    away = [d for four in AWAY for d in four]
    lines = [
        lax.ppermute(part, "z", [(i, (i + d) % NZ) for i in range(NZ)]) if d else part
        for part, d in zip(lines, away)
    ]
    early = 4
    rows_far, *lines[:early] = lax.optimization_barrier((rows_far, *lines[:early]))
    fine_far = fine(rows_far)
    lines[0], _ = lax.optimization_barrier((lines[0], fine_far))
    (own,) = run(coarse_sum_kernel, [None] * NZ, shape((16, ROWS), F32), *lines)
    last_run[0] = own
    across, following, before = (
        lax.ppermute(own, "hid", [(i, (i + d) % HID) for i in range(HID)]) for d in (2, 1, 3)
    )
    lines = [own, across, following, before]
    fine_far = swap(fine_far, "hid")
    first = scored(score_kernel, fine_near, rows_near, shape((8, LBL), F32))
    fine_far, *lines = lax.optimization_barrier((fine_far, *lines))
    table = scored(
        score_last_kernel, fine_far, rows_far, shape((HID * NX * NZ * NC * NC, 128), F32), first
    )
    table = swap(table, ("hid", "x", "z", "c"))

    loss, prob = run(
        finish_kernel,
        [smem()] + [None] * (HID + 2),
        [shape((1, ROWS), F32), shape((TOP, ROWS), F32)],
        at,
        table,
        *lines,
        routes_t,
    )
    return loss.reshape(ROWS), prob.T


def solution(mesh):
    fine_mesh = Mesh(mesh.devices.reshape(HID, NX, NZ, NC), ("hid", "x", "z", "c"))
    blk = ("x", "z", "c")
    placed = (P(blk, "hid"), P("hid", blk), P(blk, "hid", None), P(), P(blk, None), P(blk), P(blk))
    return jax.shard_map(
        local, mesh=fine_mesh, in_specs=placed, out_specs=(P(blk), P(blk, None)), check_vma=False
    )
```

```python
import jax
import jax.numpy as jnp
from jax import lax
from jax.experimental import pallas as pl
from jax.experimental.pallas import tpu as pltpu
from jax.sharding import Mesh, PartitionSpec as P

F32 = jnp.float32
BF16 = jnp.bfloat16
I32 = jnp.int32

HID, NX, NZ, NC = 4, 4, 8, 2
ROWS = 256
PART = 1024
TOP = 8
BLK = 8
QB = NC * BLK
CAP = 8
LBL = 256
INFO = 16
SLOTS = 48
TIERS = SLOTS // CAP
PAIR = 2 * CAP
WIDE = 2 * ROWS
AWAY = ((0, 1, -1, 2), (-2, 3, -3, 4))
FOUR = 2 * PAIR
ARRIVE = {0: range(0, 2), 2: range(2, BLK), BLK: range(BLK, QB)}
GROUPS = NC * NX
EXT = ROWS + INFO
VMEM = 56 * 1024 * 1024


def iota(shape, dim):
    return lax.broadcasted_iota(I32, shape, dim)


def dot(a, b):
    return jnp.dot(a, b, preferred_element_type=F32)


def strict_upper():
    return jnp.where(iota((ROWS, ROWS), 0) < iota((ROWS, ROWS), 1), 1.0, 0.0).astype(BF16)


def other(core, half):
    return core + half - 2 * core * half


def pack_kernel(f_ref, routes_ref, place_ref, offset_ref, cluster_ref, out_ref):
    out_ref[0:ROWS, :] = f_ref[...]
    routes = routes_ref[...]
    clusters = cluster_ref[...]
    count = clusters.shape[1]
    table = jnp.concatenate([clusters >> 6, clusters & 63, jnp.zeros((14, count), I32)], axis=0)
    table = table.astype(F32).astype(BF16)
    groups, columns = [], []
    blocks = iota((count, ROWS), 0)
    for k in range(TOP):
        hot = jnp.where(blocks == routes[k : k + 1, :], 1.0, 0.0).astype(BF16)
        found = dot(table, hot)
        groups.append(found[0:1, :])
        columns.append(found[1:2, :])
    places = [place_ref[...].astype(F32), offset_ref[...].astype(F32), jnp.zeros((6, ROWS), F32)]
    left = jnp.concatenate([(routes - 256).astype(F32)] + columns, axis=0)
    right = jnp.concatenate(groups + places, axis=0)
    rest = jnp.zeros((INFO, PART - WIDE), F32)
    out_ref[ROWS:EXT, :] = jnp.concatenate([left, right, rest], axis=1).astype(BF16)


def select_more_kernel(at_ref, a_ref, b_ref, begun_ref, rows_ref):
    select_kernel(at_ref, a_ref, b_ref, rows_ref)


def select_kernel(at_ref, a_ref, b_ref, rows_ref):
    z, core = at_ref[1], at_ref[2]
    count = GROUPS * BLK
    index = iota((count, ROWS), 0)
    device = ((index >> 3) & 3) * (NZ * NC) + z * NC + other(core, index >> 5)
    blocks = device * BLK + (index & 7)
    upper = strict_upper()
    ones = jnp.ones((ROWS, ROWS), BF16)
    row, col = iota((count, count), 0), iota((count, count), 1)
    before = jnp.where(((row >> 3) == (col >> 3)) & (col < row), 1.0, 0.0).astype(BF16)
    slot_of = iota((SLOTS, ROWS), 0).astype(F32)
    eye = iota((SLOTS, 128), 0) == iota((SLOTS, 128), 1)

    def as_line(column):
        return jnp.sum(jnp.where(eye, column, 0.0), axis=0, keepdims=True)

    picked, owners, places = [], [], []
    for g_ref in (a_ref, b_ref):
        info = g_ref[ROWS:EXT, 0:WIDE].astype(F32)
        routes = info[0:TOP, 0:ROWS].astype(I32) + 256
        place = info[TOP : TOP + 1, ROWS:].astype(I32)
        offset = info[TOP + 1 : TOP + 2, ROWS:]
        hit = jnp.zeros((count, ROWS), F32)
        target = jnp.zeros((1, ROWS), I32)
        for k in range(TOP):
            hit = jnp.where(routes[k : k + 1, :] == blocks, 1.0, hit)
            target = jnp.where(place == k, routes[k : k + 1, :], target)
        held = hit.astype(BF16)
        start = dot(before, dot(held, ones).astype(BF16))
        slot = jnp.where(hit > 0.5, dot(held, upper) + start, -1.0)
        wanted = jnp.where(blocks == target, slot, -1.0)
        hots = []
        for g in range(GROUPS):
            label = jnp.full((SLOTS, ROWS), -1.0, F32)
            for b in range(BLK):
                label = jnp.where(slot[g * BLK + b : g * BLK + b + 1, :] == slot_of, float(b), label)
            hots.append(jnp.where(label > -0.5, 1.0, 0.0).astype(BF16))
            owners.append(as_line(jnp.max(label, axis=1, keepdims=True)))
            mine = jnp.max(wanted[g * BLK : (g + 1) * BLK, :], axis=0, keepdims=True)
            places.append(
                as_line(
                    jnp.sum(jnp.where(mine == slot_of, offset + 1.0, 0.0), axis=1, keepdims=True)
                )
            )
        hots = jnp.concatenate(hots, axis=0)
        picked.append(dot(hots, g_ref[0:ROWS, :]).reshape(GROUPS, TIERS, CAP, PART))
    both = jnp.concatenate(picked, axis=2).astype(BF16)
    for g in range(GROUPS):
        rows_ref[g % NX, (g // NX) * TIERS : (g // NX + 1) * TIERS] = both[g]
    for d in range(NX):
        lines = []
        for half in range(NC):
            g = half * NX + d
            lines += [owners[g], owners[GROUPS + g], places[g], places[GROUPS + g]]
        lines = jnp.concatenate(lines + [jnp.zeros((8, 128), F32)], axis=0)
        lines = jnp.concatenate([lines, jnp.zeros((PAIR, PART - 128), F32)], axis=1)
        rows_ref[d, NC * TIERS] = lines.astype(BF16)


def partial_kernel(a_ref, b_ref, c_ref, d_ref, w_ref, out_ref):
    for s, ref in enumerate((a_ref, b_ref, c_ref, d_ref)):
        out_ref[:, s * ROWS : (s + 1) * ROWS] = lax.dot_general(
            w_ref[...], ref[0:ROWS, :], (((1,), (1,)), ((), ())), preferred_element_type=F32
        )


def slot_lines(meta, half, kind):
    eye = iota((SLOTS, 128), 0) == iota((SLOTS, 128), 1)
    columns = []
    for s in range(4):
        at = (s // 2) * PAIR + half * 4 + kind * 2 + s % 2
        column = jnp.sum(jnp.where(eye, meta[at : at + 1, :], 0.0), axis=1, keepdims=True)
        columns.append(jnp.broadcast_to(column, (SLOTS, LBL)))
    return jnp.concatenate(
        [c[t * CAP : (t + 1) * CAP, :] for t in range(TIERS) for c in columns], axis=0
    )


def fine_kernel(own_ref, peer_ref, r_ref, out_ref, held_ref, owner_ref, sems):
    copies = []
    for i in range(QB):
        source = own_ref if i < BLK else peer_ref
        copies.append(pltpu.make_async_copy(source.at[i % BLK], held_ref.at[i], sems.at[i]))
        copies[i].start()
    for half in range(NC):
        for x in range(NX):
            meta = r_ref[x, NC * TIERS, :, 0:128].astype(F32)
            owner_ref[x] = slot_lines(meta, half, 0).reshape(TIERS, FOUR, LBL)
        for b in range(BLK):
            for i in ARRIVE.get(half * BLK + b, ()):
                copies[i].wait()
            end = min(b + 1, TIERS)
            rows = r_ref[:, half * TIERS : half * TIERS + end].reshape(NX * end * FOUR, PART)
            part = dot(rows, held_ref[half * BLK + b])
            for x in range(NX):
                for t in range(end):
                    at = (x * end + t) * FOUR
                    piece = part[at : at + FOUR]
                    if t < b:
                        piece = jnp.where(owner_ref[x, t] == float(b), piece, out_ref[x, half, t])
                    out_ref[x, half, t] = piece


def score(y, h, meta_ref):
    rows = NC * TIERS * FOUR
    y = y.reshape(rows, LBL)
    meta = meta_ref[h, 0, :, 0:128].astype(F32)
    wanted = jnp.concatenate([slot_lines(meta, half, 1) for half in range(NC)], axis=0)
    label = iota((rows, LBL), 1).astype(F32) + 1.0
    top = jnp.max(y, axis=1, keepdims=True)
    mass = top + jnp.log(jnp.sum(jnp.exp(y - top), axis=1, keepdims=True))
    target = jnp.sum(jnp.where(label == wanted, y, 0.0), axis=1, keepdims=True)
    order = iota((rows, LBL), 0)
    tier = order // FOUR
    half = jnp.where(tier >= TIERS, 1, 0)
    slot = half * 128 + (tier - half * TIERS) * CAP + (order & 7)
    lane = iota((rows, LBL), 1)
    packed = jnp.where(lane == slot, mass, 0.0) + jnp.where(lane == slot + 64, target, 0.0)
    packed = jnp.sum(packed.reshape(NC * TIERS, 4, CAP, LBL), axis=2)
    return jnp.sum(packed, axis=0)


def score_kernel(at_ref, y_ref, meta_ref, out_ref):
    out_ref[0:4, :] = score(y_ref[0], at_ref[3], meta_ref)
    out_ref[4:8, :] = jnp.zeros((4, LBL), F32)


def score_last_kernel(at_ref, y_ref, meta_ref, first_ref, out_ref):
    z, core, h = at_ref[1], at_ref[2], at_ref[3]
    y = y_ref[0] + y_ref[1] + y_ref[2] + y_ref[3]
    last = score(y, h, meta_ref)
    out_ref[...] = jnp.zeros_like(out_ref)
    for i, lines in enumerate((first_ref, last)):
        for s in range(4):
            to = (z + NZ + AWAY[i][s]) & (NZ - 1)
            for d in range(HID):
                at = (((d * NX + h) * NZ + to) * NC + core) * NC
                for half in range(NC):
                    line = lines[s : s + 1, half * 128 : (half + 1) * 128]
                    out_ref[pl.ds(at + half, 1), :] = line


def coarse_lines(at_ref, c_ref, infos):
    z, h = at_ref[1], at_ref[3]
    width = c_ref.shape[0]
    column = iota((width, ROWS), 0)
    out = []
    for s, info_ref in enumerate(infos):
        logits = c_ref[:, s * ROWS : (s + 1) * ROWS]
        info = info_ref[...].astype(F32).astype(I32)
        inside = info[TOP : 2 * TOP, 0:ROWS]
        group = info[0:TOP, ROWS:WIDE]
        place = ((group >> 4) * NC + (group & 1)) * 64 + inside - h * width
        place = jnp.where(((group >> 1) & 7) == z, place, -1)
        top = jnp.max(logits, axis=0, keepdims=True)
        total = jnp.sum(jnp.exp(logits - top), axis=0, keepdims=True)
        lines = [top, total, jnp.zeros((6, ROWS), F32)]
        for k in range(TOP):
            lines.append(
                jnp.sum(
                    jnp.where(column == place[k : k + 1, :], logits, 0.0), axis=0, keepdims=True
                )
            )
        out.append(jnp.concatenate(lines, axis=0))
    return out


def coarse_kernel(at_ref, c_ref, i0, i1, i2, i3, out_ref):
    for s, lines in enumerate(coarse_lines(at_ref, c_ref, (i0, i1, i2, i3))):
        out_ref[s] = lines


def coarse_last_kernel(at_ref, c_ref, i0, i1, i2, i3, first_ref, *out_refs):
    last = coarse_lines(at_ref, c_ref, (i0, i1, i2, i3))
    for i, out_ref in enumerate(out_refs):
        out_ref[...] = first_ref[i] if i < NZ // 2 else last[i - NZ // 2]


def joined(shards):
    top = shards[0][0:1]
    for shard in shards[1:]:
        top = jnp.maximum(top, shard[0:1])
    sums = [shard[1:2] * jnp.exp(shard[0:1] - top) for shard in shards]
    picks = [shard[8:16] for shard in shards]
    while len(sums) > 1:
        sums = [a + b for a, b in zip(sums[0::2], sums[1::2])]
        picks = [a + b for a, b in zip(picks[0::2], picks[1::2])]
    return top, sums[0], picks[0]


def coarse_sum_kernel(*refs):
    *shard_refs, out_ref = refs
    top, total, picked = joined([ref[...] for ref in shard_refs])
    out_ref[0:8, :] = jnp.concatenate([top, total, jnp.zeros((6, ROWS), F32)], axis=0)
    out_ref[8:16, :] = picked


def finish_kernel(at_ref, fine_ref, *refs):
    *coarse_refs, routes_ref, loss_ref, prob_ref = refs
    x, core = at_ref[0], at_ref[2]
    routes = routes_ref[...]
    chips = NX * NZ
    index = iota((QB * chips, ROWS), 0)
    q = index >> 5
    block = ((index & 31) * NC + other(core, q >> 3)) * BLK + (q & 7)
    hit = jnp.zeros((QB * chips, ROWS), F32)
    for k in range(TOP):
        hit = jnp.where(routes[k : k + 1, :] == block, 1.0, hit)
    held = hit.astype(BF16)
    rank = dot(held, strict_upper())
    count = dot(held, jnp.ones((ROWS, ROWS), BF16))
    slots = []
    for half in range(NC):
        start = jnp.zeros((chips, ROWS), F32)
        for b in range(BLK):
            at = (half * BLK + b) * chips
            slots.append(rank[at : at + chips] + start)
            start = start + count[at : at + chips]
    slots = jnp.concatenate(slots, axis=0)

    table = fine_ref[pl.ds(x * (chips * NC * NC), chips * NC * NC), :]
    high = table.astype(BF16)
    rest = table - high.astype(F32)
    middle = rest.astype(BF16)
    low = (rest - middle.astype(F32)).astype(BF16)
    pieces = jnp.concatenate([high, middle, low], axis=0)
    row_of = iota((chips * NC * NC, ROWS), 0)
    lane_of = iota((128, ROWS), 0).astype(F32)
    pair = []
    target = jnp.zeros((1, ROWS), F32)
    for k in range(TOP):
        route = routes[k : k + 1, :]
        slot = jnp.sum(jnp.where(route == block, slots, 0.0), axis=0, keepdims=True)
        line = ((route >> 4) * NC + core) * NC + other(core, (route >> 3) & 1)
        hot = jnp.where(line == row_of, 1.0, 0.0).astype(BF16)
        found = lax.dot_general(
            pieces,
            jnp.concatenate([hot, hot, hot], axis=0),
            (((0,), (0,)), ((), ())),
            preferred_element_type=F32,
        )
        pair.append(jnp.sum(jnp.where(lane_of == slot, found, 0.0), axis=0, keepdims=True))
        target = target + jnp.sum(
            jnp.where(lane_of == slot + 64.0, found, 0.0), axis=0, keepdims=True
        )
    pair = jnp.concatenate(pair, axis=0)
    top = jnp.max(pair, axis=0, keepdims=True)
    fine_lse = top + jnp.log(jnp.sum(jnp.exp(pair - top), axis=0, keepdims=True))
    log_prob = pair - fine_lse
    prob = jnp.exp(log_prob)

    top, total, picked = joined([ref[...] for ref in coarse_refs])
    picked = picked - (top + jnp.log(total))
    kl = jnp.sum(prob * (log_prob - picked), axis=0, keepdims=True)
    loss_ref[...] = fine_lse - target + kl
    prob_ref[...] = prob


def params(**more):
    return pltpu.CompilerParams(vmem_limit_bytes=VMEM, **more)


def smem():
    return pl.BlockSpec(memory_space=pltpu.SMEM)


def shape(dims, kind):
    return jax.ShapeDtypeStruct(dims, kind)


def swap(value, axes, split=0):
    return lax.all_to_all(value, axes, split, split, tiled=True)


def local(features, coarse_weight, fine_weight, block_cluster, routes, target_route, target_offset):
    ax = lax.axis_index
    at = jnp.stack([ax("x"), ax("z"), ax("c"), ax("hid")]).astype(I32)
    hbm = pl.BlockSpec(memory_space=pl.ANY)
    routes_t = routes.T

    full = lambda *dims: pl.BlockSpec(dims, lambda i: (0,) * len(dims))

    def run(kernel, specs, out, *operands, out_specs=None, scratch=(), **more):
        outs = out if isinstance(out, list) else [out]
        specs = [full(*o.shape) if spec is None else spec for spec, o in zip(specs, operands)]
        return pl.pallas_call(
            kernel,
            grid=(1,),
            in_specs=specs,
            out_specs=out_specs or [full(*o.shape) for o in outs],
            out_shape=outs,
            scratch_shapes=scratch,
            compiler_params=params(),
            **more,
        )(*operands)

    (here,) = run(
        pack_kernel,
        [None] * 5,
        shape((EXT, PART), BF16),
        features,
        routes_t,
        target_route[None],
        target_offset[None],
        block_cluster[None],
    )
    up = [(i, (i + 1) % NZ) for i in range(NZ)]
    down = [(i, (i - 1) % NZ) for i in range(NZ)]
    from_up, from_down = [here], [here]
    for step in range(NZ // 2):
        if step < NZ // 2 - 1:
            from_up.append(lax.ppermute(from_up[-1], "z", down))
        from_down.append(lax.ppermute(from_down[-1], "z", up))
    peer_weight = lax.ppermute(fine_weight, "c", [(0, 1), (1, 0)])
    coarse_t = lax.all_gather(coarse_weight.T, ("x", "c"), axis=0, tiled=True)
    columns = coarse_t.shape[0]

    near = (here, from_up[1], from_down[1], from_up[2])
    far = (from_down[2], from_up[3], from_down[3], from_down[4])
    tiers = NC * TIERS + 1
    last_run = [here]

    def in_turn(call, first, *more):
        first, _ = lax.optimization_barrier((first, last_run[0]))
        outs = call(first, *more)
        last_run[0] = outs[0]
        return outs if len(outs) > 1 else outs[0]

    def select(four, *waits):
        out = shape((NX, tiers, FOUR, PART), BF16)
        block = (NX, tiers, PAIR, PART)

        def begin(a, b):
            to = pl.BlockSpec(block, lambda i: (0, 0, 0, 0))
            return run(select_kernel, [smem(), None, None], out, at, a, b, out_specs=[to])

        def end(a, b, begun):
            to = pl.BlockSpec(block, lambda i: (0, 0, 1, 0))
            specs = [smem(), None, None, hbm]
            return run(
                select_more_kernel,
                specs,
                out,
                at,
                a,
                b,
                begun,
                out_specs=[to],
                input_output_aliases={3: 0},
            )

        first = lax.optimization_barrier((four[0], waits[0]))[0]
        begun = in_turn(begin, first, four[1])
        first = lax.optimization_barrier((four[2], waits[1]))[0]
        return swap(in_turn(end, first, four[3], begun), "x")

    def partial(four, *waits):
        def call(*four):
            out = shape((columns, NX * ROWS), F32)
            return run(partial_kernel, [None] * 5, out, *four, coarse_t)

        first = lax.optimization_barrier((four[0], *waits))[0]
        out = in_turn(call, first, *four[1:])
        return lax.psum_scatter(out, "hid", scatter_dimension=0, tiled=True)

    info = pl.BlockSpec((INFO, WIDE), lambda i: (ROWS // INFO, 0))

    def coarse(kernel, part, four, out, *more):
        def call(c):
            specs = [smem(), None] + [info] * 4 + [None] * len(more)
            return run(kernel, specs, out, at, c, *four, *more)

        return in_turn(call, part)

    def fine(rows):
        def call(rows):
            return run(
                fine_kernel,
                [hbm, hbm, None],
                shape((NX, NC, TIERS, FOUR, LBL), F32),
                fine_weight,
                peer_weight,
                rows,
                scratch=[
                    pltpu.VMEM((QB, PART, LBL), BF16),
                    pltpu.VMEM((NX, TIERS, FOUR, LBL), F32),
                    pltpu.SemaphoreType.DMA((QB,)),
                ],
                cost_estimate=pl.CostEstimate(
                    flops=8 * 10**9, bytes_accessed=40 * 2**20, transcendentals=0
                ),
            )

        return in_turn(call, rows)

    meta = pl.BlockSpec((NX, 1, FOUR, PART), lambda i: (0, NC * TIERS, 0, 0))

    def scored(kernel, fine, rows, out, *before):
        def call(fine):
            specs = [smem(), None, meta] + [None] * len(before)
            return run(kernel, specs, out, at, fine, rows, *before)

        return in_turn(call, fine)

    rows_near = select(near, from_down[1], from_down[2])
    part_near = partial(near)
    rows_far = select(far, from_down[3], from_down[4])
    part_far = partial(far, rows_near)
    fine_near = lax.psum_scatter(fine(rows_near), "hid", scatter_dimension=0, tiled=True)
    lines = coarse(coarse_kernel, part_near, near, shape((NZ // 2, 16, ROWS), F32))
    lines = coarse(
        coarse_last_kernel, part_far, far, [shape((16, ROWS), F32)] * NZ, lines
    )
    away = [d for four in AWAY for d in four]
    lines = [
        lax.ppermute(part, "z", [(i, (i + d) % NZ) for i in range(NZ)]) if d else part
        for part, d in zip(lines, away)
    ]
    early = NZ
    rows_far, *lines[:early] = lax.optimization_barrier((rows_far, *lines[:early]))
    fine_far = fine(rows_far)
    lines[0], _ = lax.optimization_barrier((lines[0], fine_far))
    (own,) = run(coarse_sum_kernel, [None] * NZ, shape((16, ROWS), F32), *lines)
    last_run[0] = own
    across, following, before = (
        lax.ppermute(own, "hid", [(i, (i + d) % HID) for i in range(HID)]) for d in (2, 1, 3)
    )
    lines = [own, across, following, before]
    fine_far = swap(fine_far, "hid")
    first = scored(score_kernel, fine_near, rows_near, shape((8, LBL), F32))
    fine_far, *lines = lax.optimization_barrier((fine_far, *lines))
    table = scored(
        score_last_kernel, fine_far, rows_far, shape((HID * NX * NZ * NC * NC, 128), F32), first
    )
    table = swap(table, ("hid", "x", "z", "c"))

    loss, prob = run(
        finish_kernel,
        [smem()] + [None] * (HID + 2),
        [shape((1, ROWS), F32), shape((TOP, ROWS), F32)],
        at,
        table,
        *lines,
        routes_t,
    )
    return loss.reshape(ROWS), prob.T


def solution(mesh):
    fine_mesh = Mesh(mesh.devices.reshape(HID, NX, NZ, NC), ("hid", "x", "z", "c"))
    blk = ("x", "z", "c")
    placed = (P(blk, "hid"), P("hid", blk), P(blk, "hid", None), P(), P(blk, None), P(blk), P(blk))
    return jax.shard_map(
        local, mesh=fine_mesh, in_specs=placed, out_specs=(P(blk), P(blk, None)), check_vma=False
    )
```
